512 devices in a mesh: dp: 16 (over y, x_lo), query: 32 (over x_hi, z, core).
Axes of the slice: x: 4 (x_hi: 2, x_lo: 2; x = x_hi * 2 + x_lo), y: 8, z: 8, core: 2. Of those that a mesh axis runs over, the one named last changes fastest.
Arguments:
- activations: bfloat16 [65536, 14336], P(('dp', 'query')), may hold values from -200 to 200, as said below
- out_grads: bfloat16 [65536, 4096], P(('dp', 'query')), may hold values from -200 to 200, as said below
- in_projection: bfloat16 [64, 14336], P(None, 'query'), may hold values from -1 to 1
- out_projection: bfloat16 [64, 4096], P(None, 'query'), may hold values from -1 to 1
- lengths: int32 [4096], P(('dp', 'query')), may hold values from 1 to 16, 49152 in all
- queries: bfloat16 [1024, 4096], P('query'), may hold values from -0.09375 to 0.09375
Outputs:
- scores: float32 [4096, 1024], P(('dp', 'query'))
The draws below stay inside these ranges and needn't reach their ends.
Inputs may be any that keep to these rules, and one draw needn't show every extreme that they name: activations are finite with magnitudes below 200. out_grads are finite with magnitudes below 200. `lengths`: some example has all 16 slots live.
All inputs are finite; a program needn't handle non-finite values. No bound on the sum of `lengths` on one device may be relied on, other than what follows from the above.
Results may differ from the reference program's by a relative error of at most 0.0003.
Values may be sent and summed in bfloat16 or wider, within the bound.
A program may use at most 64 MiB of HBM per device.

```python
import math
import jax
import jax.numpy as jnp
import numpy as np
from jax import lax

D = 4096
FF = 14336
RANK = 64
SEQ = 16
TOK_DEV = 128
EXAMPLES = 4096
TOKENS = 65536
QUERIES = 1024


def row_scales(key_rows, count_rows, spread_top):
    rising = jnp.exp(jnp.log(3.0) * jnp.arange(count_rows, dtype=jnp.float32) / max(count_rows - 1, 1))
    spread = jnp.exp(jax.random.uniform(key_rows, (count_rows,), jnp.float32, 0.0, jnp.log(spread_top)))
    return rising * spread


def rough_matrix(key_base, count_rows, count_cols, col_low, col_high):
    key_rows, key_cols, key_vals = jax.random.split(key_base, 3)
    rows_scale = row_scales(key_rows, count_rows, 3.3)
    values = jnp.clip(jax.random.normal(key_vals, (count_rows, count_cols), jnp.float32), -6.0, 6.0)
    cols_scale = jnp.exp(jax.random.uniform(key_cols, (count_cols,), jnp.float32, jnp.log(col_low), jnp.log(col_high)))
    return values * rows_scale[:, None] * cols_scale[None, :]


def projection_matrix(key_base, count_cols):
    key_scale, key_vals = jax.random.split(key_base, 2)
    scales = jnp.exp(jax.random.uniform(key_scale, (RANK,), jnp.float32, jnp.log(0.3), jnp.log(3.0)))
    values = jnp.clip(jax.random.normal(key_vals, (RANK, count_cols), jnp.float32), -6.0, 6.0)
    return values * scales[:, None] / jnp.sqrt(jnp.float32(count_cols))


def draw_activations(key, part):
    key = jax.random.fold_in(key, 11)
    return rough_matrix(key, TOKENS, FF, 0.316, 3.16).astype(jnp.bfloat16)


def draw_out_grads(key, part):
    key = jax.random.fold_in(key, 23)
    return rough_matrix(key, TOKENS, D, 0.5, 2.0).astype(jnp.bfloat16)


def draw_in_projection(key, part):
    key = jax.random.fold_in(key, 37)
    return projection_matrix(key, FF).astype(jnp.bfloat16)


def draw_out_projection(key, part):
    key = jax.random.fold_in(key, 41)
    return projection_matrix(key, D).astype(jnp.bfloat16)


def level_of(rng, extent, shards, least, high):
    def one(dim, shards_of):
        draws = jax.random.uniform(jax.random.fold_in(jax.random.fold_in(rng, 6), dim), (shards_of,), jnp.float32, least / len(shards), high / len(shards))
        return jnp.repeat(jnp.exp(draws), extent[dim] // shards_of).reshape((-1,) + (1,) * (len(extent) - dim - 1))

    level = one(*shards[0])
    for cut in shards[1:]:
        level = level * one(*cut)
    return level


def length_profile(amount, total, reach, lean):
    loads = [(1 << 20) // math.isqrt(rank ** lean) + 1 for rank in range(2, amount + 1)]
    spare, given = total - reach - (amount - 1), [1] * (amount - 1)
    while spare > 0:
        candidates = [i for i in range(amount - 1) if given[i] < reach]
        mass, left = sum([loads[i] for i in candidates]), spare
        for i in candidates:
            extra = min(reach - given[i], max(1, left * loads[i] // mass), spare)
            given[i] = given[i] + extra
            spare = spare - extra
    return np.array([reach] + given)


def uneven(key, number_of, total, most, skew):
    if number_of == 2:
        one = jax.random.randint(key, (), max(1, total - most), min(most, total - 1) + 1)
        return jnp.stack([one, total - one])
    sizes = jnp.asarray(length_profile(number_of, total, most, skew), jnp.int32)
    pairs = (number_of - 1) // 2
    source_of, taker = sizes[1:1 + 2 * pairs:2], sizes[2:2 + 2 * pairs:2]
    margin = jnp.minimum(source_of - 1, most - taker)
    moved = jax.random.randint(jax.random.fold_in(key, 1), (pairs,), 0, 1 << 20) % (margin + 1)
    sizes = sizes.at[1:1 + 2 * pairs:2].set(source_of - moved).at[2:2 + 2 * pairs:2].set(taker + moved)
    return sizes[jax.random.permutation(jax.random.fold_in(key, 2), number_of)]


def bell_draw(rng, shape, deviation, limit, shards=(), held_as=jnp.bfloat16):
    values = jax.random.normal(rng, shape, jnp.float32) * deviation
    if len(shards) > 0:
        values = level_of(rng, shape, shards, -0.22, 0.18) * values
    return jnp.clip(values, min=-limit, max=limit).astype(held_as)


def setup_inputs(seed: int = 0) -> dict:
    streams_of = jax.random.split(jax.random.key(seed), 7)
    activations = draw_activations(jax.random.fold_in(streams_of[6], 71), 0)
    out_grads = draw_out_grads(jax.random.fold_in(streams_of[6], 71), 0)
    in_projection = draw_in_projection(jax.random.fold_in(streams_of[6], 71), 0)
    out_projection = draw_out_projection(jax.random.fold_in(streams_of[6], 71), 0)
    lengths = uneven(streams_of[4], EXAMPLES, EXAMPLES * SEQ * 3 // 4, SEQ, 1).astype(jnp.int32)
    queries = bell_draw(streams_of[5], (QUERIES, RANK * RANK), (RANK * RANK) ** -0.5, 0.09375, ((0, 32),))
    return dict(activations=activations, out_grads=out_grads, in_projection=in_projection, out_projection=out_projection, lengths=lengths, queries=queries)


def damped_inverse(factor):
    rank_size = factor.shape[0]
    identity = jnp.eye(rank_size, dtype=jnp.float32)
    damped = factor + 0.1 * jnp.trace(factor) / rank_size * identity
    lower_factor = jnp.linalg.cholesky(damped)
    lower_inverse = lax.linalg.triangular_solve(lower_factor, identity, left_side=True, lower=True)
    return jnp.dot(lower_inverse.T, lower_inverse, precision=lax.Precision.HIGHEST)

def project_rows(rows_all, weights):
    blocks = rows_all.reshape(-1, TOK_DEV, rows_all.shape[1])
    result = lax.map(lambda blocky: jnp.dot(blocky.astype(jnp.float32), weights.T.astype(jnp.float32), preferred_element_type=jnp.float32), blocks)
    return result.reshape(-1, weights.shape[0])

def reference(activations, out_grads, in_projection, out_projection, lengths, queries):
    positions = jnp.arange(SEQ, dtype=jnp.int32)
    live = (positions[None, :] < lengths[:, None]).astype(jnp.float32).reshape(-1, 1)
    projected_in = project_rows(activations, in_projection)
    projected_out = project_rows(out_grads, out_projection)
    in_factor = jnp.dot((projected_in * live).T, projected_in, precision=lax.Precision.HIGHEST) / TOKENS
    out_factor = jnp.dot((projected_out * live).T, projected_out, precision=lax.Precision.HIGHEST) / TOKENS
    in_inverse = damped_inverse(in_factor)
    out_inverse = damped_inverse(out_factor)
    example_grads = jnp.einsum('esi,esj->eij', (projected_out * live).reshape(-1, SEQ, RANK), projected_in.reshape(-1, SEQ, RANK), precision=lax.Precision.HIGHEST)
    left_done = jnp.einsum('ik,ekj->eij', out_inverse, example_grads, precision=lax.Precision.HIGHEST)
    preconditioned = jnp.einsum('eik,kj->eij', left_done, in_inverse, precision=lax.Precision.HIGHEST)
    preconditioned = preconditioned.reshape(-1, RANK * RANK)
    return jnp.dot(preconditioned, queries.astype(jnp.float32).T, precision=lax.Precision.HIGHEST)
```

```python
import functools

import jax
import jax.numpy as jnp
from jax import lax
from jax.experimental import pallas as pl
from jax.experimental.pallas import tpu as pltpu
from jax.sharding import PartitionSpec as P

MESH = pl.DeviceIdType.MESH
RANK = 64
SEQ = 16
TOK = 128
IN_COLS = 448
IN_PAD = 512
OUT_COLS = 128
BLK = IN_PAD + OUT_COLS
Q_ROWS = 32
NT = (((1,), (1,)), ((), ()))
NN = (((1,), (0,)), ((), ()))
HIGHEST = lax.Precision.HIGHEST


def dot(a, b, dims=NN, precision=None):
    return lax.dot_general(a, b, dims, precision=precision, preferred_element_type=jnp.float32)


def split(x):
    hi = x.astype(jnp.bfloat16)
    return hi, (x - hi.astype(jnp.float32)).astype(jnp.bfloat16)


def damped_inverses(total, tokens):
    lane = lax.broadcasted_iota(jnp.int32, (RANK, TOK), 1)
    row = lax.broadcasted_iota(jnp.int32, (RANK, TOK), 0)
    mean = total * (1.0 / tokens)
    done = []
    for work in (mean, pltpu.roll(mean, RANK, 1)):
        diagonal = row == lane
        trace = jnp.sum(jnp.where(diagonal, work, 0.0))
        work = jnp.where(lane < RANK, work, 0.0)
        done.append(jnp.where(diagonal, work + 0.1 * trace / RANK, work))
    one, two = done
    lane1 = lax.broadcasted_iota(jnp.int32, (1, TOK), 1)
    for k in range(RANK):
        new = []
        for work in (one, two):
            pivot_row = work[k : k + 1, :]
            inverse = 1.0 / pivot_row[:, k : k + 1]
            scaled = jnp.where(lane1 == k, inverse, pivot_row * inverse)
            update = jnp.where(lane == k, 0.0, work) - work[:, k : k + 1] * scaled
            new.append(jnp.where(row == k, scaled, update))
        one, two = new
    return one, two


def kernel(
    Y, Z, tokens,
    acts_hbm, outg_hbm, inp_ref, outp_ref, len_ref, q_hbm,
    out_ref,
    acts, outg, qraw, stage, gath, qall, tok, part, total, ar1, ar2, ar3, mine, gsc, sco, ret,
    loc_sem, z_send, z_recv, cx_send, cx_recv, pt_send, pt_recv, sb_send, sb_recv,
    t_send, t_recv, q_send, q_recv, a_send, a_recv,
):
    H = Z // 2
    dpi, qi = lax.axis_index("dp"), lax.axis_index("query")
    y, xl = dpi // 2, dpi % 2
    xh, z, c = qi // (2 * Z), (qi // 2) % Z, qi % 2

    def at(y_, xl_, xh_, z_, c_):
        return (y_ * 2 + xl_, xh_ * (2 * Z) + z_ * 2 + c_)

    def zp(off):
        return (z + (off + Z)) % Z

    def z_peer(off):
        return at(y, xl, xh, zp(off), c)

    def y_peer(off):
        return at((y + off) % Y, xl, xh, z, c)

    def x_peer(m):
        return at(y, (xl + (m // 2) % 2) % 2, (xh + m // 4) % 2, z, (c + m % 2) % 2)

    cross = at(y, 1 - xl, 1 - xh, z, c)
    partner = at(y, 1 - xl, xh, z, c)
    sibling = at(y, xl, xh, z, 1 - c)

    pending = []

    def push(ref_src, ref_dst, send, recv, to):
        copy = pltpu.make_async_remote_copy(
            src_ref=ref_src, dst_ref=ref_dst, send_sem=send, recv_sem=recv, device_id=to, device_id_type=MESH
        )
        copy.start()
        pending.append(copy)

    def got(ref, sem):
        pltpu.make_async_copy(ref, ref, sem).wait()

    loads = [
        pltpu.make_async_copy(acts_hbm, acts, loc_sem.at[0]),
        pltpu.make_async_copy(outg_hbm, outg, loc_sem.at[1]),
        pltpu.make_async_copy(q_hbm, qraw, loc_sem.at[2]),
    ]
    for load in loads:
        load.start()
    barrier = pltpu.get_barrier_semaphore()
    peers = [z_peer(d) for d in range(1, Z)] + [x_peer(m) for m in range(1, 8)] + [y_peer(d) for d in range(1, Y)]
    for peer in peers:
        pl.semaphore_signal(barrier, inc=1, device_id=peer, device_id_type=MESH)

    def block_of(h, zz, cc):
        return h * (2 * Z) + zz * 2 + cc

    def whole(b):
        return gath.at[pl.ds(pl.multiple_of(b * RANK, RANK), RANK), :]

    def piece(b, p):
        return gath.at[pl.ds(pl.multiple_of(b * RANK + p * 32, 32), 32), :]

    own = block_of(xh, z, c)
    stage[...] = jnp.zeros_like(stage)
    stage[:, 0:IN_COLS] = inp_ref[...].astype(jnp.float32)
    plain = stage[...]
    shifted = pltpu.roll(plain, IN_PAD - IN_COLS, 1)
    own_rows = pl.ds(pl.multiple_of(own * RANK, RANK), RANK)
    gath[own_rows, 0:IN_PAD] = jnp.where(c == 1, shifted, plain).astype(jnp.bfloat16)
    gath[own_rows, IN_PAD:BLK] = outp_ref[...]
    pl.semaphore_wait(barrier, len(peers))

    offs = [0]
    for s in range(1, H):
        offs += [-s, s]
    offs.append(H)

    def z_forward(k, ref_of, send, recv):
        off = offs[k]
        dist = abs(off)
        for way, sign in ((0, 1), (1, -1)):
            goes = (k == 0) or (k != Z - 1 and (off < 0) == (sign > 0))
            if not goes:
                continue
            for p in (0, 1):
                if dist + 1 == H and p != way:
                    continue
                ref = ref_of(zp(off), p)
                push(ref, ref, send.at[way, dist, p], recv.at[way, dist, p], z_peer(sign))

    def z_wait(k, ref_of, recv):
        off = offs[k]
        dist = abs(off)
        if dist == 0:
            return
        for p in (0, 1):
            if dist == H:
                way = p
            else:
                way = 0 if off < 0 else 1
            got(ref_of(zp(off), p), recv.at[way, dist - 1, p])

    def gath_piece(zz, p):
        return piece(block_of(xh, zz, c), p)

    sums = [jnp.zeros((RANK, TOK), jnp.float32), jnp.zeros((RANK, TOK), jnp.float32)]

    def fold(h, zz, cc):
        b = block_of(h, zz, cc)
        rows = pl.ds(pl.multiple_of(b * RANK, RANK), RANK)
        first = pl.multiple_of((h * Z + zz) * (2 * IN_COLS) + cc * 384, 128)
        sums[0] = sums[0] + dot(gath[rows, 0:IN_PAD], acts[:, pl.ds(first, IN_PAD)], NT)
        second = pl.multiple_of(b * OUT_COLS, OUT_COLS)
        sums[1] = sums[1] + dot(gath[rows, IN_PAD:BLK], outg[:, pl.ds(second, OUT_COLS)], NT)

    for tick in range(Z + 4):
        if tick < Z:
            zz = zp(offs[tick])
            z_wait(tick, gath_piece, z_recv)
            z_forward(tick, gath_piece, z_send, z_recv)
            ref = piece(block_of(xh, zz, c), xl)
            push(ref, ref, cx_send.at[tick], cx_recv.at[tick], cross)
            ref = whole(block_of(xh, zz, c))
            push(ref, ref, sb_send.at[tick, 0], sb_recv.at[tick, 0], sibling)
        k = tick - 1
        if 0 <= k < Z:
            ref = piece(block_of(1 - xh, zp(offs[k]), c), 1 - xl)
            got(ref, cx_recv.at[k])
            push(ref, ref, pt_send.at[k], pt_recv.at[k], partner)
            push(ref, ref, sb_send.at[k, 1], sb_recv.at[k, 1], sibling)
        k = tick - 2
        if 0 <= k < Z:
            ref = piece(block_of(1 - xh, zp(offs[k]), c), xl)
            got(ref, pt_recv.at[k])
            push(ref, ref, sb_send.at[k, 2], sb_recv.at[k, 2], sibling)
        if tick == 0:
            loads[0].wait()
            loads[1].wait()
        if tick < Z:
            fold(xh, zp(offs[tick]), c)
        k = tick - 2
        if 0 <= k < Z:
            zz = zp(offs[k])
            fold(1 - xh, zz, c)
            got(whole(block_of(xh, zz, 1 - c)), sb_recv.at[k, 0])
            fold(xh, zz, 1 - c)
        k = tick - 4
        if 0 <= k < Z:
            zz = zp(offs[k])
            got(piece(block_of(1 - xh, zz, 1 - c), 1 - xl), sb_recv.at[k, 1])
            got(piece(block_of(1 - xh, zz, 1 - c), xl), sb_recv.at[k, 2])
            fold(1 - xh, zz, 1 - c)

    lane1 = lax.broadcasted_iota(jnp.int32, (1, TOK), 1)
    counts = jnp.zeros((1, TOK), jnp.int32)
    for e in range(TOK // SEQ):
        counts = jnp.where(lane1 // SEQ == e, len_ref[e], counts)
    live = (lane1 % SEQ < counts).astype(jnp.float32)
    masked = jnp.concatenate(sums, axis=0) * live
    own_tok = pl.ds(pl.multiple_of(z * TOK, TOK), TOK)
    tok[own_tok, :] = masked
    gram = dot(masked, masked, NT, HIGHEST)
    lane = lax.broadcasted_iota(jnp.int32, (RANK, TOK), 1)
    part[...] = jnp.where(lane < RANK, gram[0:RANK], gram[RANK:])

    rows_z = RANK // Z

    def z_rows(zz):
        return pl.ds(pl.multiple_of(zz * rows_z, rows_z), rows_z)

    def tok_piece(zz, p):
        return tok.at[pl.ds(pl.multiple_of(zz * TOK + p * RANK, RANK), RANK), :]

    def tok_step(k):
        z_wait(k, tok_piece, t_recv)
        z_forward(k, tok_piece, t_send, t_recv)

    for d in range(1, Z):
        push(part.at[z_rows(zp(d)), :], ar1.at[d - 1], a_send.at[0, d - 1], a_recv.at[0], z_peer(d))
    tok_step(0)
    lane_q = lax.broadcasted_iota(jnp.int32, (Q_ROWS, TOK), 1)
    loads[2].wait()
    q_cols = qraw.shape[1]

    def q_slot(h, cc):
        return (h * 2 + cc) * Q_ROWS

    def q_piece(h, cc, p):
        half = Q_ROWS // 2
        return qall.at[pl.ds(pl.multiple_of(q_slot(h, cc) + p * half, half), half), :]

    own_q = pl.ds(pl.multiple_of(q_slot(xh, c), Q_ROWS), Q_ROWS)
    for m in range(q_cols // 256):
        first = qraw[:, 128 * m : 128 * m + 128].astype(jnp.float32)
        second = qraw[:, q_cols // 2 + 128 * m : q_cols // 2 + 128 * m + 128].astype(jnp.float32)
        low = jnp.where(lane_q < RANK, first, pltpu.roll(second, RANK, 1))
        high = jnp.where(lane_q < RANK, pltpu.roll(first, RANK, 1), second)
        qall[own_q, 256 * m : 256 * m + 128] = low.astype(jnp.bfloat16)
        qall[own_q, 256 * m + 128 : 256 * m + 256] = high.astype(jnp.bfloat16)
    ref = q_piece(xh, c, xl)
    push(ref, ref, q_send.at[0], q_recv.at[0], cross)
    ref = qall.at[own_q, :]
    push(ref, ref, q_send.at[1], q_recv.at[1], sibling)

    got(ar1, a_recv.at[0])
    summed = part[z_rows(z), :]
    for d in range(Z - 1):
        summed = summed + ar1[d]
    mine[0] = summed
    for m in range(1, 8):
        push(mine.at[0], ar2.at[m - 1], a_send.at[1, m - 1], a_recv.at[1], x_peer(m))
    for k in range(1, min(3, Z)):
        tok_step(k)
    got(ar2, a_recv.at[1])
    for m in range(7):
        summed = summed + ar2[m]
    mine[1] = summed
    for d in range(1, Y):
        push(mine.at[1], ar3.at[d - 1], a_send.at[2, d - 1], a_recv.at[2], y_peer(d))
    for k in range(3, min(5, Z)):
        tok_step(k)
    got(ar3, a_recv.at[2])
    for d in range(Y - 1):
        summed = summed + ar3[d]
    total[z_rows(z), :] = summed
    for d in range(1, Z):
        here = total.at[z_rows(z), :]
        push(here, here, a_send.at[3, d - 1], a_recv.at[3], z_peer(d))
    for k in range(5, Z):
        tok_step(k)
    ref = q_piece(1 - xh, c, 1 - xl)
    got(ref, q_recv.at[0])
    push(ref, ref, q_send.at[2], q_recv.at[2], partner)
    push(ref, ref, q_send.at[3], q_recv.at[3], sibling)
    got(total.at[0 : RANK - rows_z, :], a_recv.at[3])

    in_inverse, out_inverse = damped_inverses(total[...], tokens)

    ref = q_piece(1 - xh, c, xl)
    got(ref, q_recv.at[2])
    push(ref, ref, q_send.at[4], q_recv.at[4], sibling)

    example = lax.broadcasted_iota(jnp.int32, (SEQ // 2, TOK), 0)
    token = lax.broadcasted_iota(jnp.int32, (SEQ // 2, TOK), 1)
    belongs = (token // SEQ == example).astype(jnp.float32)
    nothing = jnp.zeros((RANK, TOK), jnp.bfloat16)
    half = RANK // 2
    for k in range(Z):
        ins = dot(in_inverse[:, 0:RANK], tok[k * TOK : k * TOK + RANK, :], NN, HIGHEST)
        outs = dot(out_inverse[:, 0:RANK], tok[k * TOK + RANK : (k + 1) * TOK, :], NN, HIGHEST)
        left, right = [], []
        for w in split(outs):
            spread = (w.astype(jnp.float32)[:, None, :] * belongs[None, :, :]).astype(jnp.bfloat16)
            spread = spread.reshape(RANK * 8, TOK)
            left.append(jnp.concatenate([spread[0 : half * 8], spread[half * 8 :]], axis=1))
        for w in split(ins):
            right.append(
                jnp.concatenate(
                    [jnp.concatenate([w, nothing], axis=1), jnp.concatenate([nothing, w], axis=1)], axis=0
                )
            )
        grads = dot(left[0], right[0], NT) + (dot(left[0], right[1], NT) + dot(left[1], right[0], NT))
        gsc[:, k * 8 : (k + 1) * 8, :] = grads.reshape(half, 8, TOK)

    got(qall.at[pl.ds(pl.multiple_of(q_slot(xh, 1 - c), Q_ROWS), Q_ROWS), :], q_recv.at[1])
    got(q_piece(1 - xh, 1 - c, 1 - xl), q_recv.at[3])
    got(q_piece(1 - xh, 1 - c, xl), q_recv.at[4])
    scores = jnp.zeros((2 * 8 * Z, TOK), jnp.float32)
    for m in range(half // 2):
        both = jnp.concatenate([gsc[2 * m], gsc[2 * m + 1]], axis=1)
        hi, lo = split(both)
        scores = scores + dot(jnp.concatenate([hi, lo], axis=0), qall[:, 256 * m : 256 * m + 256], NT)
    sco[...] = scores[0 : 8 * Z] + scores[8 * Z :]
    for d in range(1, Z):
        push(
            sco.at[pl.ds(pl.multiple_of(zp(d) * 8, 8), 8), :], ret.at[d], a_send.at[4, d - 1], a_recv.at[4], z_peer(d)
        )
    ret[0] = sco[pl.ds(pl.multiple_of(z * 8, 8), 8), :]
    got(ret.at[1:Z], a_recv.at[4])
    lane8 = lax.broadcasted_iota(jnp.int32, (8, TOK), 1)
    width = Z * RANK
    for m in range(Z // 2):
        first = ret[zp(-2 * m)]
        second = ret[zp(-2 * m - 1)]
        out_ref[:, 128 * m : 128 * m + 128] = jnp.where(lane8 < RANK, first, pltpu.roll(second, RANK, 1))
        out_ref[:, width + 128 * m : width + 128 * m + 128] = jnp.where(
            lane8 < RANK, pltpu.roll(first, RANK, 1), second
        )
    for copy in pending:
        copy.wait_send()


def solution(mesh):
    Y, Z = mesh.shape["dp"] // 2, mesh.shape["query"] // 4
    H = Z // 2

    def on_device(activations, out_grads, in_projection, out_projection, lengths, queries):
        tokens = activations.shape[0] * mesh.shape["dp"] * mesh.shape["query"]
        f32, bf16 = jnp.float32, jnp.bfloat16
        vmem = pl.BlockSpec(memory_space=pltpu.VMEM)
        hbm = pl.BlockSpec(memory_space=pl.ANY)
        sem = pltpu.SemaphoreType.DMA
        return pl.pallas_call(
            functools.partial(kernel, Y, Z, tokens),
            out_shape=jax.ShapeDtypeStruct((lengths.shape[0], Z * 4 * Q_ROWS), f32),
            in_specs=[hbm, hbm, vmem, vmem, pl.BlockSpec(memory_space=pltpu.SMEM), hbm],
            out_specs=vmem,
            scratch_shapes=[
                pltpu.VMEM(activations.shape, bf16),
                pltpu.VMEM(out_grads.shape, bf16),
                pltpu.VMEM(queries.shape, bf16),
                pltpu.VMEM((RANK, IN_PAD), f32),
                pltpu.VMEM((4 * Z * RANK, BLK), bf16),
                pltpu.VMEM((4 * Q_ROWS, queries.shape[1]), bf16),
                pltpu.VMEM((Z * TOK, TOK), f32),
                pltpu.VMEM((RANK, TOK), f32),
                pltpu.VMEM((RANK, TOK), f32),
                pltpu.VMEM((Z - 1, RANK // Z, TOK), f32),
                pltpu.VMEM((7, RANK // Z, TOK), f32),
                pltpu.VMEM((Y - 1, RANK // Z, TOK), f32),
                pltpu.VMEM((2, RANK // Z, TOK), f32),
                pltpu.VMEM((RANK // 2, 8 * Z, TOK), f32),
                pltpu.VMEM((8 * Z, TOK), f32),
                pltpu.VMEM((Z, 8, TOK), f32),
                sem((3,)),
                sem((2, H, 2)),
                sem((2, H, 2)),
                sem((Z,)),
                sem((Z,)),
                sem((Z,)),
                sem((Z,)),
                sem((Z, 3)),
                sem((Z, 3)),
                sem((2, H, 2)),
                sem((2, H, 2)),
                sem((5,)),
                sem((5,)),
                sem((5, 7)),
                sem((5,)),
            ],
            compiler_params=pltpu.CompilerParams(
                collective_id=0, has_side_effects=True, vmem_limit_bytes=50 * 1024 * 1024
            ),
        )(activations, out_grads, in_projection, out_projection, lengths, queries)

    placed = (
        P(("dp", "query"), None),
        P(("dp", "query"), None),
        P(None, "query"),
        P(None, "query"),
        P(("dp", "query")),
        P("query", None),
    )
    return jax.shard_map(
        on_device, mesh=mesh, in_specs=placed, out_specs=P(("dp", "query"), None), check_vma=False
    )
```

```python
import functools
import heapq

import jax
import jax.numpy as jnp
from jax import lax
from jax.experimental import pallas as pl
from jax.experimental.pallas import tpu as pltpu
from jax.sharding import PartitionSpec as P

MESH = pl.DeviceIdType.MESH
RANK = 64
SEQ = 16
TOK = 128
IN_COLS = 448
IN_PAD = 512
OUT_COLS = 128
BLK = IN_PAD + OUT_COLS
Q_ROWS = 32
NT = (((1,), (1,)), ((), ()))
NN = (((1,), (0,)), ((), ()))
HIGHEST = lax.Precision.HIGHEST


def dot(a, b, dims=NN, precision=None):
    return lax.dot_general(a, b, dims, precision=precision, preferred_element_type=jnp.float32)


def split(x):
    hi = x.astype(jnp.bfloat16)
    return hi, (x - hi.astype(jnp.float32)).astype(jnp.bfloat16)


def damped_inverses(total, tokens):
    lane = lax.broadcasted_iota(jnp.int32, (RANK, TOK), 1)
    row = lax.broadcasted_iota(jnp.int32, (RANK, TOK), 0)
    mean = total * (1.0 / tokens)
    done = []
    for work in (mean, pltpu.roll(mean, RANK, 1)):
        diagonal = row == lane
        trace = jnp.sum(jnp.where(diagonal, work, 0.0))
        work = jnp.where(lane < RANK, work, 0.0)
        done.append(jnp.where(diagonal, work + 0.1 * trace / RANK, work))
    one, two = done
    lane1 = lax.broadcasted_iota(jnp.int32, (1, TOK), 1)
    for k in range(RANK):
        new = []
        for work in (one, two):
            pivot_row = work[k : k + 1, :]
            inverse = 1.0 / pivot_row[:, k : k + 1]
            scaled = jnp.where(lane1 == k, inverse, pivot_row * inverse)
            update = jnp.where(lane == k, 0.0, work) - work[:, k : k + 1] * scaled
            new.append(jnp.where(row == k, scaled, update))
        one, two = new
    return one, two


def gather_order(Z):
    H = Z // 2
    latency, send_time, lag = 2.3, 0.8, 0.6
    free, heap, order, held = {}, [], [], {}

    def send(t, link, event):
        start = max(t, free.get(link, 0.0))
        free[link] = start + send_time
        heapq.heappush(heap, (start + send_time + latency, len(free) + len(order), len(heap), event))

    def arrived(t, kind, way, dist, part):
        order.append((t, len(order), (kind, way, dist, part)))
        if kind == "z":
            for to in (0, 1) if dist == 0 else (way,):
                if goes_on(H, dist, to, part):
                    send(t, to, ("z", to, dist + 1, part))
            if part == 0:
                send(t, "c", ("c", way, dist, part))
        elif kind == "c":
            send(t, "p", ("p", way, dist, part))
        name = (kind != "z", 0 if dist == H else way, dist)
        held[name] = held.get(name, 0) + 1
        if held[name] == 2:
            order.append((t + lag, len(order), ("fold",) + name))

    arrived(0.0, "z", 0, 0, 0)
    arrived(0.0, "z", 0, 0, 1)
    while heap:
        t, _, _, event = heapq.heappop(heap)
        arrived(t, *event)
    return [event for _, _, event in sorted(order)]


def goes_on(H, dist, way, part):
    return dist + 1 < H or (dist + 1 == H and part == way)


def kernel(
    Y, Z, tokens,
    acts_hbm, outg_hbm, inp_hbm, outp_hbm, len_hbm, q_hbm,
    out_ref,
    acts, outg, inp, outp, lens, qraw, stage, gath, halves, other, qall, tok, part, total, ar1, ar2, ar3, mine, gsc, sco, ret,
    loc_sem, act_loc, act_send, act_recv, og_sem, z_send, z_recv, cx_send, cx_recv, pt_send, pt_recv, sw_sem,
    t_send, t_recv, q_send, q_recv, a_send, a_recv,
):
    H = Z // 2
    dpi, qi = lax.axis_index("dp"), lax.axis_index("query")
    y, xl = dpi // 2, dpi % 2
    xh, z, c = qi // (2 * Z), (qi // 2) % Z, qi % 2

    def at(y_, xl_, xh_, z_, c_):
        return (y_ * 2 + xl_, xh_ * (2 * Z) + z_ * 2 + c_)

    def zp(off):
        return (z + (off + Z)) % Z

    def z_peer(off):
        return at(y, xl, xh, zp(off), c)

    def y_peer(off):
        return at((y + off) % Y, xl, xh, z, c)

    def x_peer(m):
        return at(y, (xl + (m // 2) % 2) % 2, (xh + m // 4) % 2, z, (c + m % 2) % 2)

    cross = at(y, 1 - xl, 1 - xh, z, c)
    partner = at(y, 1 - xl, xh, z, c)
    sibling = at(y, xl, xh, z, 1 - c)

    pending = []

    def push(ref_src, ref_dst, send, recv, to):
        copy = pltpu.make_async_remote_copy(
            src_ref=ref_src, dst_ref=ref_dst, send_sem=send, recv_sem=recv, device_id=to, device_id_type=MESH
        )
        copy.start()
        pending.append(copy)

    def got(ref, sem):
        pltpu.make_async_copy(ref, ref, sem).wait()

    barrier = pltpu.get_barrier_semaphore()
    peers = [z_peer(d) for d in range(1, Z)] + [x_peer(m) for m in range(1, 8)] + [y_peer(d) for d in range(1, Y)]
    for peer in peers:
        pl.semaphore_signal(barrier, inc=1, device_id=peer, device_id_type=MESH)

    loads = [
        pltpu.make_async_copy(inp_hbm, inp, loc_sem.at[0]),
        pltpu.make_async_copy(outp_hbm, outp, loc_sem.at[1]),
        pltpu.make_async_copy(q_hbm, qraw, loc_sem.at[2]),
        pltpu.make_async_copy(len_hbm, lens, loc_sem.at[3]),
    ]
    for load in loads:
        load.start()

    order = gather_order(Z)
    folds = [event for event in order if event[0] == "fold"]

    def off_of(way, dist):
        return dist if way == 1 else -dist

    def window(far, way, dist):
        return ((1 - xh) if far else xh) * Z + zp(off_of(way, dist))

    def act_columns(k, cc):
        return pl.ds(pl.multiple_of(k * (2 * IN_COLS) + cc * (IN_COLS - RANK), 128), IN_PAD)

    def act_slot(k, cc):
        return acts.at[pl.ds(pl.multiple_of(cc * TOK, TOK), TOK), pl.ds(pl.multiple_of(k * IN_PAD, IN_PAD), IN_PAD)]

    def out_slot(cc):
        return outg.at[pl.ds(pl.multiple_of(cc * TOK, TOK), TOK), :]

    own_loads = []
    for j, (_, far, way, dist) in enumerate(folds):
        k = window(far, way, dist)
        own_loads.append(pltpu.make_async_copy(acts_hbm.at[:, act_columns(k, c)], act_slot(k, c), act_loc.at[j]))
        own_loads[-1].start()
        if j == 0:
            out_load = pltpu.make_async_copy(outg_hbm, out_slot(c), og_sem.at[0])
            out_load.start()

    def piece(h, zz, p):
        return gath.at[pl.ds(pl.multiple_of((h * Z + zz) * RANK + p * 32, 32), 32), :]

    stage[...] = jnp.zeros_like(stage)
    loads[0].wait()
    loads[1].wait()
    stage[:, 0:IN_COLS] = inp[...].astype(jnp.float32)
    plain = stage[...]
    shifted = pltpu.roll(plain, IN_PAD - IN_COLS, 1)
    own_rows = pl.ds(pl.multiple_of((xh * Z + z) * RANK, RANK), RANK)
    gath[own_rows, 0:IN_PAD] = jnp.where(c == 1, shifted, plain).astype(jnp.bfloat16)
    gath[own_rows, IN_PAD:BLK] = outp[...]
    pl.semaphore_wait(barrier, len(peers))

    lane_q = lax.broadcasted_iota(jnp.int32, (Q_ROWS, TOK), 1)
    q_cols = qraw.shape[1]

    def q_slot(h, cc):
        return (h * 2 + cc) * Q_ROWS

    def q_piece(h, cc, p):
        half = Q_ROWS // 2
        return qall.at[pl.ds(pl.multiple_of(q_slot(h, cc) + p * half, half), half), :]

    own_q = pl.ds(pl.multiple_of(q_slot(xh, c), Q_ROWS), Q_ROWS)

    def pair_queries():
        loads[2].wait()
        for m in range(q_cols // 256):
            first = qraw[:, 128 * m : 128 * m + 128].astype(jnp.float32)
            second = qraw[:, q_cols // 2 + 128 * m : q_cols // 2 + 128 * m + 128].astype(jnp.float32)
            low = jnp.where(lane_q < RANK, first, pltpu.roll(second, RANK, 1))
            high = jnp.where(lane_q < RANK, pltpu.roll(first, RANK, 1), second)
            qall[own_q, 256 * m : 256 * m + 128] = low.astype(jnp.bfloat16)
            qall[own_q, 256 * m + 128 : 256 * m + 256] = high.astype(jnp.bfloat16)

    sums = [jnp.zeros((RANK, 2 * TOK), jnp.float32), jnp.zeros((RANK, 2 * TOK), jnp.float32)]
    first_fold = True
    for event in order:
        kind, rest = event[0], event[1:]
        if kind == "z":
            way, dist, p = rest
            ref = piece(xh, zp(off_of(way, dist)), xl if p == 0 else 1 - xl)
            if dist > 0:
                got(ref, z_recv.at[way, dist - 1, p])
            for to in (0, 1) if dist == 0 else (way,):
                if goes_on(H, dist, to, p):
                    push(ref, ref, z_send.at[to, dist, p], z_recv.at[to, dist, p], z_peer(1 if to == 0 else -1))
            if p == 0:
                push(ref, ref, cx_send.at[way, dist], cx_recv.at[way, dist], cross)
        elif kind == "c":
            way, dist, _ = rest
            ref = piece(1 - xh, zp(off_of(way, dist)), 1 - xl)
            got(ref, cx_recv.at[way, dist])
            push(ref, ref, pt_send.at[way, dist], pt_recv.at[way, dist], partner)
        elif kind == "p":
            way, dist, _ = rest
            got(piece(1 - xh, zp(off_of(way, dist)), xl), pt_recv.at[way, dist])
        else:
            far, way, dist = rest
            if first_fold:
                first_fold = False
                for j, (_, far_, way_, dist_) in enumerate(folds):
                    k = window(far_, way_, dist_)
                    push(acts_hbm.at[:, act_columns(k, 1 - c)], act_slot(k, c), act_send.at[j], act_recv.at[j], sibling)
                    if j == 0:
                        push(outg_hbm, out_slot(c), og_sem.at[1], og_sem.at[2], sibling)
                pair_queries()
                out_load.wait()
                got(out_slot(1 - c), og_sem.at[2])
            j = folds.index(event)
            k = window(far, way, dist)
            own_loads[j].wait()
            got(act_slot(k, 1 - c), act_recv.at[j])
            rows = pl.ds(pl.multiple_of(k * RANK, RANK), RANK)
            columns = pl.ds(pl.multiple_of(k * IN_PAD, IN_PAD), IN_PAD)
            sums[0] = sums[0] + dot(gath[rows, 0:IN_PAD], acts[:, columns], NT)
            columns = pl.ds(pl.multiple_of(k * (2 * OUT_COLS) + c * OUT_COLS, OUT_COLS), OUT_COLS)
            sums[1] = sums[1] + dot(gath[rows, IN_PAD:BLK], outg[:, columns], NT)

    ref = q_piece(xh, c, xl)
    push(ref, ref, q_send.at[0], q_recv.at[0], cross)
    for cc in range(2):
        halves[cc] = jnp.concatenate([sums[0][:, cc * TOK : (cc + 1) * TOK], sums[1][:, cc * TOK : (cc + 1) * TOK]], axis=0)
    push(halves.at[1 - c], other, sw_sem.at[0], sw_sem.at[1], sibling)
    ref = qall.at[own_q, :]
    push(ref, ref, q_send.at[1], q_recv.at[1], sibling)

    lane1 = lax.broadcasted_iota(jnp.int32, (1, TOK), 1)
    counts = jnp.zeros((1, TOK), jnp.int32)
    loads[3].wait()
    for e in range(TOK // SEQ):
        counts = jnp.where(lane1 // SEQ == e, lens[e], counts)
    live = (lane1 % SEQ < counts).astype(jnp.float32)
    got(other, sw_sem.at[1])
    masked = (halves[c] + other[...]) * live
    own_tok = pl.ds(pl.multiple_of(z * TOK, TOK), TOK)
    tok[own_tok, :] = masked
    gram = dot(masked, masked, NT, HIGHEST)
    lane = lax.broadcasted_iota(jnp.int32, (RANK, TOK), 1)
    part[...] = jnp.where(lane < RANK, gram[0:RANK], gram[RANK:])

    rows_z = RANK // Z

    def z_rows(zz):
        return pl.ds(pl.multiple_of(zz * rows_z, rows_z), rows_z)

    def tok_piece(zz, p):
        return tok.at[pl.ds(pl.multiple_of(zz * TOK + p * RANK, RANK), RANK), :]

    def tok_step(dist):
        for way, sign in ((0, -1), (1, 1)):
            for p in (0, 1):
                ref = tok_piece(zp(sign * dist), p)
                if dist == H and p != way:
                    continue
                if dist > 0:
                    got(ref, t_recv.at[way, dist - 1, p])
                if goes_on(H, dist, way, p):
                    push(ref, ref, t_send.at[way, dist, p], t_recv.at[way, dist, p], z_peer(-sign))

    for d in range(1, Z):
        push(part.at[z_rows(zp(d)), :], ar1.at[d - 1], a_send.at[0, d - 1], a_recv.at[0], z_peer(d))
    tok_step(0)
    got(ar1, a_recv.at[0])
    summed = part[z_rows(z), :]
    for d in range(Z - 1):
        summed = summed + ar1[d]
    mine[0] = summed
    for d in range(1, Y):
        push(mine.at[0], ar2.at[d - 1], a_send.at[1, d - 1], a_recv.at[1], y_peer(d))
    tok_step(1)
    ref = q_piece(1 - xh, c, 1 - xl)
    got(ref, q_recv.at[0])
    push(ref, ref, q_send.at[2], q_recv.at[2], partner)
    push(ref, ref, q_send.at[3], q_recv.at[3], sibling)
    got(ar2, a_recv.at[1])
    for d in range(Y - 1):
        summed = summed + ar2[d]
    mine[1] = summed
    for m in range(1, 8):
        push(mine.at[1], ar3.at[m - 1], a_send.at[2, m - 1], a_recv.at[2], x_peer(m))
    if H > 2:
        tok_step(2)
    got(ar3, a_recv.at[2])
    for m in range(7):
        summed = summed + ar3[m]
    total[z_rows(z), :] = summed
    for d in range(1, Z):
        here = total.at[z_rows(z), :]
        push(here, here, a_send.at[3, d - 1], a_recv.at[3], z_peer(d))
    if H > 3:
        tok_step(3)
    ref = q_piece(1 - xh, c, xl)
    got(ref, q_recv.at[2])
    push(ref, ref, q_send.at[4], q_recv.at[4], sibling)
    got(total.at[0 : RANK - rows_z, :], a_recv.at[3])

    in_inverse, out_inverse = damped_inverses(total[...], tokens)

    if H > 1:
        tok_step(H)

    example = lax.broadcasted_iota(jnp.int32, (SEQ // 2, TOK), 0)
    token = lax.broadcasted_iota(jnp.int32, (SEQ // 2, TOK), 1)
    belongs = (token // SEQ == example).astype(jnp.float32)
    nothing = jnp.zeros((RANK, TOK), jnp.bfloat16)
    half = RANK // 2
    for k in range(Z):
        ins = dot(in_inverse[:, 0:RANK], tok[k * TOK : k * TOK + RANK, :], NN, HIGHEST)
        outs = dot(out_inverse[:, 0:RANK], tok[k * TOK + RANK : (k + 1) * TOK, :], NN, HIGHEST)
        left, right = [], []
        for w in split(outs):
            spread = (w.astype(jnp.float32)[:, None, :] * belongs[None, :, :]).astype(jnp.bfloat16)
            spread = spread.reshape(RANK * 8, TOK)
            left.append(jnp.concatenate([spread[0 : half * 8], spread[half * 8 :]], axis=1))
        for w in split(ins):
            right.append(
                jnp.concatenate(
                    [jnp.concatenate([w, nothing], axis=1), jnp.concatenate([nothing, w], axis=1)], axis=0
                )
            )
        grads = dot(left[0], right[0], NT) + (dot(left[0], right[1], NT) + dot(left[1], right[0], NT))
        gsc[:, k * 8 : (k + 1) * 8, :] = grads.reshape(half, 8, TOK)

    got(qall.at[pl.ds(pl.multiple_of(q_slot(xh, 1 - c), Q_ROWS), Q_ROWS), :], q_recv.at[1])
    got(q_piece(1 - xh, 1 - c, 1 - xl), q_recv.at[3])
    got(q_piece(1 - xh, 1 - c, xl), q_recv.at[4])
    scores = jnp.zeros((2 * 8 * Z, TOK), jnp.float32)
    for m in range(half // 2):
        both = jnp.concatenate([gsc[2 * m], gsc[2 * m + 1]], axis=1)
        hi, lo = split(both)
        scores = scores + dot(jnp.concatenate([hi, lo], axis=0), qall[:, 256 * m : 256 * m + 256], NT)
    sco[...] = scores[0 : 8 * Z] + scores[8 * Z :]
    for d in range(1, Z):
        push(
            sco.at[pl.ds(pl.multiple_of(zp(d) * 8, 8), 8), :], ret.at[d], a_send.at[4, d - 1], a_recv.at[4], z_peer(d)
        )
    ret[0] = sco[pl.ds(pl.multiple_of(z * 8, 8), 8), :]
    got(ret.at[1:Z], a_recv.at[4])
    lane8 = lax.broadcasted_iota(jnp.int32, (8, TOK), 1)
    width = Z * RANK
    for m in range(Z // 2):
        first = ret[zp(-2 * m)]
        second = ret[zp(-2 * m - 1)]
        out_ref[:, 128 * m : 128 * m + 128] = jnp.where(lane8 < RANK, first, pltpu.roll(second, RANK, 1))
        out_ref[:, width + 128 * m : width + 128 * m + 128] = jnp.where(
            lane8 < RANK, pltpu.roll(first, RANK, 1), second
        )
    for copy in pending:
        copy.wait_send()


def solution(mesh):
    Y, Z = mesh.shape["dp"] // 2, mesh.shape["query"] // 4
    H = Z // 2

    def on_device(activations, out_grads, in_projection, out_projection, lengths, queries):
        tokens = activations.shape[0] * mesh.shape["dp"] * mesh.shape["query"]
        f32, bf16 = jnp.float32, jnp.bfloat16
        sem = pltpu.SemaphoreType.DMA
        return pl.pallas_call(
            functools.partial(kernel, Y, Z, tokens),
            out_shape=jax.ShapeDtypeStruct((lengths.shape[0], Z * 4 * Q_ROWS), f32),
            in_specs=[pl.BlockSpec(memory_space=pltpu.HBM)] * 6,
            out_specs=pl.BlockSpec(memory_space=pltpu.VMEM),
            scratch_shapes=[
                pltpu.VMEM((2 * TOK, 2 * Z * IN_PAD), bf16),
                pltpu.VMEM((2 * TOK, out_grads.shape[1]), bf16),
                pltpu.VMEM(in_projection.shape, bf16),
                pltpu.VMEM(out_projection.shape, bf16),
                pltpu.SMEM(lengths.shape, jnp.int32),
                pltpu.VMEM(queries.shape, bf16),
                pltpu.VMEM((RANK, IN_PAD), f32),
                pltpu.VMEM((2 * Z * RANK, BLK), bf16),
                pltpu.VMEM((2, TOK, TOK), f32),
                pltpu.VMEM((TOK, TOK), f32),
                pltpu.VMEM((4 * Q_ROWS, queries.shape[1]), bf16),
                pltpu.VMEM((Z * TOK, TOK), f32),
                pltpu.VMEM((RANK, TOK), f32),
                pltpu.VMEM((RANK, TOK), f32),
                pltpu.VMEM((Z - 1, RANK // Z, TOK), f32),
                pltpu.VMEM((Y - 1, RANK // Z, TOK), f32),
                pltpu.VMEM((7, RANK // Z, TOK), f32),
                pltpu.VMEM((2, RANK // Z, TOK), f32),
                pltpu.VMEM((RANK // 2, 8 * Z, TOK), f32),
                pltpu.VMEM((8 * Z, TOK), f32),
                pltpu.VMEM((Z, 8, TOK), f32),
                sem((4,)),
                sem((2 * Z,)),
                sem((2 * Z,)),
                sem((2 * Z,)),
                sem((3,)),
                sem((2, H, 2)),
                sem((2, H, 2)),
                sem((2, H + 1)),
                sem((2, H + 1)),
                sem((2, H + 1)),
                sem((2, H + 1)),
                sem((2,)),
                sem((2, H, 2)),
                sem((2, H, 2)),
                sem((5,)),
                sem((5,)),
                sem((5, 7)),
                sem((5,)),
            ],
            compiler_params=pltpu.CompilerParams(
                collective_id=0, has_side_effects=True, vmem_limit_bytes=60 * 1024 * 1024
            ),
        )(activations, out_grads, in_projection, out_projection, lengths, queries)

    placed = (
        P(("dp", "query"), None),
        P(("dp", "query"), None),
        P(None, "query"),
        P(None, "query"),
        P(("dp", "query")),
        P("query", None),
    )
    return jax.shard_map(
        on_device, mesh=mesh, in_specs=placed, out_specs=P(("dp", "query"), None), check_vma=False
    )
```

```python
import functools

import jax
import jax.numpy as jnp
from jax import lax
from jax.experimental import pallas as pl
from jax.experimental.pallas import tpu as pltpu
from jax.sharding import PartitionSpec as P

MESH = pl.DeviceIdType.MESH
RANK = 64
SEQ = 16
TOK = 128
IN_COLS = 448
IN_PAD = 512
OUT_COLS = 128
BLK = IN_PAD + OUT_COLS
Q_ROWS = 32
NT = (((1,), (1,)), ((), ()))
NN = (((1,), (0,)), ((), ()))


def dot(a, b, dims=NN):
    return lax.dot_general(a, b, dims, preferred_element_type=jnp.float32)


def split(x):
    hi = x.astype(jnp.bfloat16)
    return hi, (x - hi.astype(jnp.float32)).astype(jnp.bfloat16)


def inverse_of_four(p):
    a, b, d = p[0][0], p[0][1], p[1][1]
    scale = 1.0 / (a * d - b * b)
    u00, u01, u11 = d * scale, -b * scale, a * scale
    c = [[p[0][2], p[0][3]], [p[1][2], p[1][3]]]
    x = [[u00 * c[0][j] + u01 * c[1][j] for j in range(2)], [u01 * c[0][j] + u11 * c[1][j] for j in range(2)]]
    s00 = p[2][2] - (c[0][0] * x[0][0] + c[1][0] * x[1][0])
    s01 = p[2][3] - (c[0][0] * x[0][1] + c[1][0] * x[1][1])
    s11 = p[3][3] - (c[0][1] * x[0][1] + c[1][1] * x[1][1])
    scale = 1.0 / (s00 * s11 - s01 * s01)
    t00, t01, t11 = s11 * scale, -s01 * scale, s00 * scale
    w = [[x[i][0] * t00 + x[i][1] * t01, x[i][0] * t01 + x[i][1] * t11] for i in range(2)]
    v00 = u00 + w[0][0] * x[0][0] + w[0][1] * x[0][1]
    v01 = u01 + w[0][0] * x[1][0] + w[0][1] * x[1][1]
    v11 = u11 + w[1][0] * x[1][0] + w[1][1] * x[1][1]
    return [
        [v00, v01, -w[0][0], -w[0][1]],
        [v01, v11, -w[1][0], -w[1][1]],
        [-w[0][0], -w[1][0], t00, t01],
        [-w[0][1], -w[1][1], t01, t11],
    ]


def damped_inverses(total, tokens):
    lane = lax.broadcasted_iota(jnp.int32, (RANK, TOK), 1)
    row = lax.broadcasted_iota(jnp.int32, (RANK, TOK), 0)
    column = lane % RANK
    left = lane < RANK
    work = total * (1.0 / tokens)
    diagonal = jnp.where(column == row, work, 0.0)
    trace = jnp.where(left, jnp.sum(jnp.where(left, diagonal, 0.0)), jnp.sum(jnp.where(left, 0.0, diagonal)))
    work = jnp.where(column == row, work + 0.1 * trace / RANK, work)
    first = jnp.where(left, 0, RANK)
    column1 = lax.broadcasted_iota(jnp.int32, (1, TOK), 1) % RANK
    for k in range(0, RANK, 4):
        columns = [jnp.take_along_axis(work, first + (k + i), axis=1) for i in range(4)]
        rows = [work[k + i : k + i + 1] for i in range(4)]
        pivot = inverse_of_four([[columns[j][k + i : k + i + 1] for j in range(4)] for i in range(4)])
        scaled = []
        for i in range(4):
            value = (pivot[i][0] * rows[0] + pivot[i][1] * rows[1]) + (pivot[i][2] * rows[2] + pivot[i][3] * rows[3])
            for j in range(4):
                value = jnp.where(column1 == k + j, pivot[i][j], value)
            scaled.append(value)
        work = jnp.where((column >= k) & (column < k + 4), 0.0, work)
        work = (work - columns[0] * scaled[0] - columns[1] * scaled[1]) - (
            columns[2] * scaled[2] + columns[3] * scaled[3]
        )
        for i in range(4):
            work = jnp.where(row == k + i, scaled[i], work)
    return work


def gather_order(Z):
    H = Z // 2
    times = {d: 4.5 + 0.95 * (H - 1 - d) for d in range(1, H)}
    times[H] = max(times.get(H - 1, 4.5) + 2.5, 7.0)
    order = [(0.3, "near", 0), (5.0, "q", 0), (9.4, "q", 1)]
    for off in [0] + [sign * d for d in range(H - 1, 0, -1) for sign in (-1, 1)] + [H]:
        t = times[abs(off)] if off else 0.0
        if off:
            order += [(t, "z", off), (t + 2.7, "y", off), (t + 2.75, "near", off)]
        order += [(t + 2.7, "c", off), (t + 5.2, "p", off), (t + 5.3, "far", off)]
    return [event[1:] for event in sorted(order, key=lambda event: event[0])]


def goes_on(H, dist, way, part):
    return dist + 1 < H or (dist + 1 == H and part == way)


def kernel(
    Y, Z, tokens,
    acts_hbm, outg_hbm, inp_hbm, outp_hbm, len_hbm, q_hbm,
    out_ref,
    acts, outg, inp, outp, lens, qraw, stage, gath, halves, other, both, spare, lives, qall, tok, part, total, ar1, ar2, ar3, mine, gsc, sco, ret,
    loc_sem, act_loc, act_send, act_recv, og_sem, z_send, z_recv, r_send, r_recv, y_send, y_recv, cx_send, cx_recv,
    pt_send, pt_recv, sw_sem,
    t_send, t_recv, q_send, q_recv, a_send, a_recv,
):
    H = Z // 2
    dpi, qi = lax.axis_index("dp"), lax.axis_index("query")
    y, xl = dpi // 2, dpi % 2
    xh, z, c = qi // (2 * Z), (qi // 2) % Z, qi % 2

    def at(y_, xl_, xh_, z_, c_):
        return (y_ * 2 + xl_, xh_ * (2 * Z) + z_ * 2 + c_)

    def zp(off):
        return (z + (off + Z)) % Z

    def z_peer(off):
        return at(y, xl, xh, zp(off), c)

    def y_peer(off):
        return at((y + off) % Y, xl, xh, z, c)

    def x_peer(m):
        return at(y, (xl + (m // 2) % 2) % 2, (xh + m // 4) % 2, z, (c + m % 2) % 2)

    cross = at(y, 1 - xl, 1 - xh, z, c)
    partner = at(y, 1 - xl, xh, z, c)
    sibling = at(y, xl, xh, z, 1 - c)

    pending = []

    def push(ref_src, ref_dst, send, recv, to):
        copy = pltpu.make_async_remote_copy(
            src_ref=ref_src, dst_ref=ref_dst, send_sem=send, recv_sem=recv, device_id=to, device_id_type=MESH
        )
        copy.start()
        pending.append(copy)

    def got(ref, sem):
        pltpu.make_async_copy(ref, ref, sem).wait()

    loads = [
        pltpu.make_async_copy(inp_hbm, inp, loc_sem.at[0]),
        pltpu.make_async_copy(outp_hbm, outp, loc_sem.at[1]),
        pltpu.make_async_copy(q_hbm, qraw, loc_sem.at[2]),
        pltpu.make_async_copy(len_hbm, lens, loc_sem.at[3]),
    ]
    for load in loads:
        load.start()

    barrier = pltpu.get_barrier_semaphore()
    peers = [y_peer(d) for d in range(1, Y)] + [z_peer(d) for d in range(1, Z)] + [x_peer(m) for m in range(7, 0, -1)]
    for peer in peers:
        pl.semaphore_signal(barrier, inc=1, device_id=peer, device_id_type=MESH)

    order = gather_order(Z)
    folds = [event for event in order if event[0] in ("near", "far")]

    def window(name, off):
        return (xh if name == "near" else 1 - xh) * Z + zp(off)

    def act_columns(k, cc):
        return pl.ds(pl.multiple_of(k * (2 * IN_COLS) + cc * (IN_COLS - RANK), 128), IN_PAD)

    def act_slot(k, cc):
        return acts.at[pl.ds(pl.multiple_of(cc * TOK, TOK), TOK), pl.ds(pl.multiple_of(k * IN_PAD, IN_PAD), IN_PAD)]

    def out_slot(cc):
        return outg.at[pl.ds(pl.multiple_of(cc * TOK, TOK), TOK), :]

    mate = at(y + 1 - 2 * (y % 2), xl, xh, z, c)
    side = (y + xl) % 2

    def piece(h, off, p):
        return gath.at[pl.ds(pl.multiple_of((h * Z + zp(off)) * RANK + p * 32, 32), 32), :]

    def quarter(off, r):
        return gath.at[pl.ds(pl.multiple_of((xh * Z + zp(off)) * RANK + side * 32 + r * 16, 16), 16), :]

    stage[...] = jnp.zeros_like(stage)
    loads[0].wait()
    loads[1].wait()
    stage[:, 0:IN_COLS] = inp[...].astype(jnp.float32)
    plain = stage[...]
    shifted = pltpu.roll(plain, IN_PAD - IN_COLS, 1)
    own_rows = pl.ds(pl.multiple_of((xh * Z + z) * RANK, RANK), RANK)
    gath[own_rows, 0:IN_PAD] = jnp.where(c == 1, shifted, plain).astype(jnp.bfloat16)
    gath[own_rows, IN_PAD:BLK] = outp[...]
    pl.semaphore_wait(barrier, len(peers))

    lane_q = lax.broadcasted_iota(jnp.int32, (Q_ROWS, TOK), 1)
    q_cols = qraw.shape[1]

    def q_slot(h, cc):
        return (h * 2 + cc) * Q_ROWS

    def q_piece(h, cc, p):
        half = Q_ROWS // 2
        return qall.at[pl.ds(pl.multiple_of(q_slot(h, cc) + p * half, half), half), :]

    own_q = pl.ds(pl.multiple_of(q_slot(xh, c), Q_ROWS), Q_ROWS)

    def pair_queries():
        loads[2].wait()
        for m in range(q_cols // 256):
            first = qraw[:, 128 * m : 128 * m + 128].astype(jnp.float32)
            second = qraw[:, q_cols // 2 + 128 * m : q_cols // 2 + 128 * m + 128].astype(jnp.float32)
            low = jnp.where(lane_q < RANK, first, pltpu.roll(second, RANK, 1))
            high = jnp.where(lane_q < RANK, pltpu.roll(first, RANK, 1), second)
            qall[own_q, 256 * m : 256 * m + 128] = low.astype(jnp.bfloat16)
            qall[own_q, 256 * m + 128 : 256 * m + 256] = high.astype(jnp.bfloat16)

    sums = [jnp.zeros((RANK, 2 * TOK), jnp.float32), jnp.zeros((RANK, 2 * TOK), jnp.float32)]
    ref = piece(xh, 0, side)
    for d in range(H - 1, 0, -1):
        for sign in (1, -1):
            push(ref, ref, z_send.at[H - 1 + sign * d], z_recv.at[H - 1 - sign * d], z_peer(sign * d))
    push(ref, ref, cx_send.at[H - 1], cx_recv.at[H - 1], cross)
    own_loads = []
    for j, fold in enumerate(folds):
        k = window(*fold)
        own_loads.append(pltpu.make_async_copy(acts_hbm.at[:, act_columns(k, c)], act_slot(k, c), act_loc.at[j]))
        own_loads[-1].start()
        if j == 0:
            out_load = pltpu.make_async_copy(outg_hbm, out_slot(c), og_sem.at[0])
            out_load.start()
    for event in order:
        kind, off = event
        slot = H - 1 + off
        if kind == "z":
            ref = piece(xh, off, side)
            if off == H:
                got(quarter(H, 0), r_recv.at[0])
                got(quarter(H, 1), r_recv.at[1])
            else:
                got(ref, z_recv.at[slot])
            for r, sign in ((0, 1), (1, -1)):
                if off == -sign * (H - 1):
                    relay = quarter(off, r)
                    push(relay, relay, r_send.at[r], r_recv.at[r], z_peer(sign))
            push(ref, ref, cx_send.at[slot], cx_recv.at[slot], cross)
            push(ref, ref, y_send.at[slot], y_recv.at[slot], mate)
        elif kind == "y":
            got(piece(xh, off, 1 - side), y_recv.at[slot])
        elif kind == "c":
            ref = piece(1 - xh, off, 1 - side)
            got(ref, cx_recv.at[slot])
            push(ref, ref, pt_send.at[slot], pt_recv.at[slot], partner)
        elif kind == "p":
            got(piece(1 - xh, off, side), pt_recv.at[slot])
        elif event == ("q", 0):
            ref = q_piece(1 - xh, c, 1 - xl)
            got(ref, q_recv.at[0])
            push(ref, ref, q_send.at[2], q_recv.at[2], partner)
            push(ref, ref, q_send.at[3], q_recv.at[3], sibling)
        elif event == ("q", 1):
            ref = q_piece(1 - xh, c, xl)
            got(ref, q_recv.at[2])
            push(ref, ref, q_send.at[4], q_recv.at[4], sibling)
        else:
            j = folds.index(event)
            if j == 0:
                for i, fold in enumerate(folds):
                    k = window(*fold)
                    push(acts_hbm.at[:, act_columns(k, 1 - c)], act_slot(k, c), act_send.at[i], act_recv.at[i], sibling)
                    if i == 0:
                        push(outg_hbm, out_slot(c), og_sem.at[1], og_sem.at[2], sibling)
                pair_queries()
                ref = q_piece(xh, c, xl)
                push(ref, ref, q_send.at[0], q_recv.at[0], cross)
                ref = qall.at[own_q, :]
                push(ref, ref, q_send.at[1], q_recv.at[1], sibling)
                lane1 = lax.broadcasted_iota(jnp.int32, (8, TOK), 1)
                counts = jnp.zeros((8, TOK), jnp.int32)
                loads[3].wait()
                for e in range(TOK // SEQ):
                    counts = jnp.where(lane1 // SEQ == e, lens[e], counts)
                lives[c] = (lane1 % SEQ < counts).astype(jnp.float32)
                push(lives.at[c], lives.at[c], sw_sem.at[2], sw_sem.at[3], sibling)
                out_load.wait()
                got(out_slot(1 - c), og_sem.at[2])
            k = window(*event)
            own_loads[j].wait()
            got(act_slot(k, 1 - c), act_recv.at[j])
            rows = pl.ds(pl.multiple_of(k * RANK, RANK), RANK)
            columns = pl.ds(pl.multiple_of(k * IN_PAD, IN_PAD), IN_PAD)
            sums[0] = sums[0] + dot(gath[rows, 0:IN_PAD], acts[:, columns], NT)
            columns = pl.ds(pl.multiple_of(k * (2 * OUT_COLS) + c * OUT_COLS, OUT_COLS), OUT_COLS)
            sums[1] = sums[1] + dot(gath[rows, IN_PAD:BLK], outg[:, columns], NT)

    halves[0] = sums[0]
    halves[1] = sums[1]
    push(halves.at[1 - c], other, sw_sem.at[0], sw_sem.at[1], sibling)
    got(lives.at[1 - c], sw_sem.at[3])
    live = jnp.concatenate([lives[0, 0:1, :], lives[1, 0:1, :]], axis=1)
    got(other, sw_sem.at[1])
    masked = (halves[c] + other[...]) * live
    both[...] = masked
    hi, lo = split(masked)
    hi_lo = jnp.concatenate([hi, lo], axis=1)
    twice = jnp.concatenate([hi_lo, hi_lo], axis=0)
    lo_hi = jnp.concatenate([lo, hi], axis=1)
    gram = dot(hi_lo, twice, NT) + dot(lo_hi, twice, NT)
    half = RANK // 2
    lane = lax.broadcasted_iota(jnp.int32, (half, TOK), 1)
    part[...] = jnp.where(lane < RANK, gram[0:half], gram[half:])

    rows_x = half // 4

    def x_rows(m):
        index = ((xh + m // 4) % 2) * 2 + (xl + (m // 2) % 2) % 2
        return pl.ds(pl.multiple_of(index * rows_x, rows_x), rows_x)

    def tok_piece(zz, p):
        return tok.at[pl.ds(pl.multiple_of(zz * TOK + p * RANK, RANK), RANK), :]

    def tok_step(dist):
        for way, sign in ((0, -1), (1, 1)):
            for p in (0, 1):
                ref = tok_piece(zp(sign * dist), p)
                if dist == H and p != way:
                    continue
                if dist > 0:
                    got(ref, t_recv.at[way, dist - 1, p])
                if goes_on(H, dist, way, p):
                    push(ref, ref, t_send.at[way, dist, p], t_recv.at[way, dist, p], z_peer(-sign))

    for j, m in enumerate((4, 6, 2)):
        push(part.at[x_rows(m), :], ar1.at[j], a_send.at[0, j], a_recv.at[0], x_peer(m))
    for cc in range(2):

        @pl.when(c == cc)
        def _():
            tok[pl.ds(pl.multiple_of(z * TOK + cc * RANK, RANK), RANK), :] = both[:, cc * TOK : (cc + 1) * TOK]
            spare[...] = both[:, (1 - cc) * TOK : (2 - cc) * TOK]

    push(spare, tok_piece(z, c), sw_sem.at[4], sw_sem.at[5], sibling)
    got(ar1, a_recv.at[0])
    summed = part[x_rows(0), :]
    for j in range(3):
        summed = summed + ar1[j]
    mine[0] = summed
    for d in range(1, Z):
        push(mine.at[0], ar2.at[d - 1], a_send.at[1, d - 1], a_recv.at[1], z_peer(d))
    got(tok_piece(z, 1 - c), sw_sem.at[5])
    tok_step(0)
    tok_step(1)
    got(ar2, a_recv.at[1])
    for d in range(Z - 1):
        summed = summed + ar2[d]
    mine[1] = summed
    for d in range(1, Y):
        push(mine.at[1], ar3.at[d - 1], a_send.at[2, d - 1], a_recv.at[2], y_peer(d))
    if H > 2:
        tok_step(2)
    got(ar3, a_recv.at[2])
    for d in range(Y - 1):
        summed = summed + ar3[d]

    def total_rows(cc):
        return total.at[pl.ds(pl.multiple_of((cc * 4 + xh * 2 + xl) * rows_x, rows_x), rows_x), :]

    here = total_rows(c)
    here[...] = summed
    for m in (5, 7, 4, 6, 3, 2, 1):
        push(here, here, a_send.at[3, m - 1], a_recv.at[3], x_peer(m))
    if H > 3:
        tok_step(3)
    got(total.at[0 : RANK - rows_x, :], a_recv.at[3])
    if H > 1:
        tok_step(H)

    ins, outs = total[0:half], total[half:]
    sides = jnp.concatenate(
        [
            jnp.where(lane < RANK, ins, pltpu.roll(outs, RANK, 1)),
            jnp.where(lane < RANK, pltpu.roll(ins, RANK, 1), outs),
        ],
        axis=0,
    )
    inverses = damped_inverses(sides, tokens)
    lane = lax.broadcasted_iota(jnp.int32, (RANK, TOK), 1)
    blocks = jnp.concatenate(
        [jnp.where(lane < RANK, inverses, 0.0), jnp.where(lane < RANK, 0.0, inverses)], axis=0
    )
    hi, lo = split(blocks)
    blocks = jnp.concatenate([hi, lo, hi], axis=1)
    example = lax.broadcasted_iota(jnp.int32, (SEQ // 2, TOK), 0)
    token = lax.broadcasted_iota(jnp.int32, (SEQ // 2, TOK), 1)
    belongs = (token // SEQ == example).astype(jnp.float32)
    nothing = jnp.zeros((RANK, TOK), jnp.bfloat16)
    for k in range(Z):
        if k % 2 == 0:
            rows = [split(tok[(k + i) * TOK : (k + i + 1) * TOK, :]) for i in range(2)]
            hi = jnp.concatenate([rows[0][0], rows[1][0]], axis=1)
            lo = jnp.concatenate([rows[0][1], rows[1][1]], axis=1)
            pair = dot(blocks, jnp.concatenate([hi, hi, lo], axis=0))
        ins, outs = pair[0:RANK, (k % 2) * TOK : (k % 2 + 1) * TOK], pair[RANK:, (k % 2) * TOK : (k % 2 + 1) * TOK]
        left, right = [], []
        for w in split(outs):
            spread = (w.astype(jnp.float32)[:, None, :] * belongs[None, :, :]).astype(jnp.bfloat16)
            spread = spread.reshape(RANK * 8, TOK)
            left.append(jnp.concatenate([spread[0 : half * 8], spread[half * 8 :]], axis=1))
        for w in split(ins):
            right += [jnp.concatenate([w, nothing], axis=1), jnp.concatenate([nothing, w], axis=1)]
        grads = dot(left[0], jnp.concatenate(right, axis=0), NT)
        grads = grads[:, 0:TOK] + (grads[:, TOK:] + dot(left[1], jnp.concatenate(right[0:2], axis=0), NT))
        gsc[:, k * 8 : (k + 1) * 8, :] = grads.reshape(half, 8, TOK)

    got(qall.at[pl.ds(pl.multiple_of(q_slot(xh, 1 - c), Q_ROWS), Q_ROWS), :], q_recv.at[1])
    got(q_piece(1 - xh, 1 - c, 1 - xl), q_recv.at[3])
    got(q_piece(1 - xh, 1 - c, xl), q_recv.at[4])
    scores = jnp.zeros((2 * 8 * Z, TOK), jnp.float32)
    for m in range(half // 2):
        both = jnp.concatenate([gsc[2 * m], gsc[2 * m + 1]], axis=1)
        hi, lo = split(both)
        scores = scores + dot(jnp.concatenate([hi, lo], axis=0), qall[:, 256 * m : 256 * m + 256], NT)
    sco[...] = scores[0 : 8 * Z] + scores[8 * Z :]
    for d in range(1, Z):
        push(
            sco.at[pl.ds(pl.multiple_of(zp(d) * 8, 8), 8), :], ret.at[d], a_send.at[4, d - 1], a_recv.at[4], z_peer(d)
        )
    ret[0] = sco[pl.ds(pl.multiple_of(z * 8, 8), 8), :]
    got(ret.at[1:Z], a_recv.at[4])
    lane8 = lax.broadcasted_iota(jnp.int32, (8, TOK), 1)
    width = Z * RANK
    for m in range(Z // 2):
        first = ret[zp(-2 * m)]
        second = ret[zp(-2 * m - 1)]
        out_ref[:, 128 * m : 128 * m + 128] = jnp.where(lane8 < RANK, first, pltpu.roll(second, RANK, 1))
        out_ref[:, width + 128 * m : width + 128 * m + 128] = jnp.where(
            lane8 < RANK, pltpu.roll(first, RANK, 1), second
        )
    for copy in pending:
        copy.wait_send()


def solution(mesh):
    Y, Z = mesh.shape["dp"] // 2, mesh.shape["query"] // 4
    H = Z // 2

    def on_device(activations, out_grads, in_projection, out_projection, lengths, queries):
        tokens = activations.shape[0] * mesh.shape["dp"] * mesh.shape["query"]
        f32, bf16 = jnp.float32, jnp.bfloat16
        sem = pltpu.SemaphoreType.DMA
        return pl.pallas_call(
            functools.partial(kernel, Y, Z, tokens),
            out_shape=jax.ShapeDtypeStruct((lengths.shape[0], Z * 4 * Q_ROWS), f32),
            in_specs=[pl.BlockSpec(memory_space=pltpu.HBM)] * 6,
            out_specs=pl.BlockSpec(memory_space=pltpu.VMEM),
            scratch_shapes=[
                pltpu.VMEM((2 * TOK, 2 * Z * IN_PAD), bf16),
                pltpu.VMEM((2 * TOK, out_grads.shape[1]), bf16),
                pltpu.VMEM(in_projection.shape, bf16),
                pltpu.VMEM(out_projection.shape, bf16),
                pltpu.SMEM(lengths.shape, jnp.int32),
                pltpu.VMEM(queries.shape, bf16),
                pltpu.VMEM((RANK, IN_PAD), f32),
                pltpu.VMEM((2 * Z * RANK, BLK), bf16),
                pltpu.VMEM((2, RANK, 2 * TOK), f32),
                pltpu.VMEM((RANK, 2 * TOK), f32),
                pltpu.VMEM((RANK, 2 * TOK), f32),
                pltpu.VMEM((RANK, TOK), f32),
                pltpu.VMEM((2, 8, TOK), f32),
                pltpu.VMEM((4 * Q_ROWS, queries.shape[1]), bf16),
                pltpu.VMEM((Z * TOK, TOK), f32),
                pltpu.VMEM((RANK // 2, TOK), f32),
                pltpu.VMEM((RANK, TOK), f32),
                pltpu.VMEM((3, RANK // 8, TOK), f32),
                pltpu.VMEM((Z - 1, RANK // 8, TOK), f32),
                pltpu.VMEM((Y - 1, RANK // 8, TOK), f32),
                pltpu.VMEM((2, RANK // 8, TOK), f32),
                pltpu.VMEM((RANK // 2, 8 * Z, TOK), f32),
                pltpu.VMEM((8 * Z, TOK), f32),
                pltpu.VMEM((Z, 8, TOK), f32),
                sem((4,)),
                sem((2 * Z,)),
                sem((2 * Z,)),
                sem((2 * Z,)),
                sem((3,)),
                sem((Z,)),
                sem((Z,)),
                sem((2,)),
                sem((2,)),
                sem((Z,)),
                sem((Z,)),
                sem((Z,)),
                sem((Z,)),
                sem((Z,)),
                sem((Z,)),
                sem((6,)),
                sem((2, H, 2)),
                sem((2, H, 2)),
                sem((5,)),
                sem((5,)),
                sem((5, 7)),
                sem((5,)),
            ],
            compiler_params=pltpu.CompilerParams(
                collective_id=0, has_side_effects=True, vmem_limit_bytes=60 * 1024 * 1024
            ),
        )(activations, out_grads, in_projection, out_projection, lengths, queries)

    placed = (
        P(("dp", "query"), None),
        P(("dp", "query"), None),
        P(None, "query"),
        P(None, "query"),
        P(("dp", "query")),
        P("query", None),
    )
    return jax.shard_map(
        on_device, mesh=mesh, in_specs=placed, out_specs=P(("dp", "query"), None), check_vma=False
    )
```

```python
import functools

import jax
import jax.numpy as jnp
from jax import lax
from jax.experimental import pallas as pl
from jax.experimental.pallas import tpu as pltpu
from jax.sharding import PartitionSpec as P

MESH = pl.DeviceIdType.MESH
RANK = 64
SEQ = 16
TOK = 128
IN_COLS = 448
IN_PAD = 512
OUT_COLS = 128
FULL = 384
HALF = RANK // 2
PIECE = 4 * HALF + HALF // 2
Q_ROWS = 32
NT = (((1,), (1,)), ((), ()))
NN = (((1,), (0,)), ((), ()))


def dot(a, b, dims=NN):
    return lax.dot_general(a, b, dims, preferred_element_type=jnp.float32)


def split(x):
    hi = x.astype(jnp.bfloat16)
    return hi, (x - hi.astype(jnp.float32)).astype(jnp.bfloat16)


def inverse_of_four(p):
    a, b, d = p[0][0], p[0][1], p[1][1]
    scale = 1.0 / (a * d - b * b)
    u00, u01, u11 = d * scale, -b * scale, a * scale
    c = [[p[0][2], p[0][3]], [p[1][2], p[1][3]]]
    x = [[u00 * c[0][j] + u01 * c[1][j] for j in range(2)], [u01 * c[0][j] + u11 * c[1][j] for j in range(2)]]
    s00 = p[2][2] - (c[0][0] * x[0][0] + c[1][0] * x[1][0])
    s01 = p[2][3] - (c[0][0] * x[0][1] + c[1][0] * x[1][1])
    s11 = p[3][3] - (c[0][1] * x[0][1] + c[1][1] * x[1][1])
    scale = 1.0 / (s00 * s11 - s01 * s01)
    t00, t01, t11 = s11 * scale, -s01 * scale, s00 * scale
    w = [[x[i][0] * t00 + x[i][1] * t01, x[i][0] * t01 + x[i][1] * t11] for i in range(2)]
    v00 = u00 + w[0][0] * x[0][0] + w[0][1] * x[0][1]
    v01 = u01 + w[0][0] * x[1][0] + w[0][1] * x[1][1]
    v11 = u11 + w[1][0] * x[1][0] + w[1][1] * x[1][1]
    return [
        [v00, v01, -w[0][0], -w[0][1]],
        [v01, v11, -w[1][0], -w[1][1]],
        [-w[0][0], -w[1][0], t00, t01],
        [-w[0][1], -w[1][1], t01, t11],
    ]


def damped_inverses(total, tokens):
    lane = lax.broadcasted_iota(jnp.int32, (RANK, TOK), 1)
    row = lax.broadcasted_iota(jnp.int32, (RANK, TOK), 0)
    column = lane % RANK
    left = lane < RANK
    work = total * (1.0 / tokens)
    diagonal = jnp.where(column == row, work, 0.0)
    trace = jnp.where(left, jnp.sum(jnp.where(left, diagonal, 0.0)), jnp.sum(jnp.where(left, 0.0, diagonal)))
    work = jnp.where(column == row, work + 0.1 * trace / RANK, work)
    first = jnp.where(left, 0, RANK)
    column1 = lax.broadcasted_iota(jnp.int32, (1, TOK), 1) % RANK
    for k in range(0, RANK, 4):
        columns = [jnp.take_along_axis(work, first + (k + i), axis=1) for i in range(4)]
        rows = [work[k + i : k + i + 1] for i in range(4)]
        pivot = inverse_of_four([[columns[j][k + i : k + i + 1] for j in range(4)] for i in range(4)])
        scaled = []
        for i in range(4):
            value = (pivot[i][0] * rows[0] + pivot[i][1] * rows[1]) + (pivot[i][2] * rows[2] + pivot[i][3] * rows[3])
            for j in range(4):
                value = jnp.where(column1 == k + j, pivot[i][j], value)
            scaled.append(value)
        work = jnp.where((column >= k) & (column < k + 4), 0.0, work)
        work = (work - columns[0] * scaled[0] - columns[1] * scaled[1]) - (
            columns[2] * scaled[2] + columns[3] * scaled[3]
        )
        for i in range(4):
            work = jnp.where(row == k + i, scaled[i], work)
    return work


def gather_order(Z):
    H = Z // 2
    times = {d: 4.5 + 0.95 * (H - 1 - d) for d in range(1, H)}
    times[H] = max(times.get(H - 1, 4.5) + 2.5, 7.0)
    order = [(0.3, "near", 0), (5.0, "q", 0), (9.4, "q", 1)]
    for off in [0] + [sign * d for d in range(H - 1, 0, -1) for sign in (-1, 1)] + [H]:
        t = times[abs(off)] if off else 0.0
        if off:
            order += [(t, "z", off), (t + 2.7, "y", off), (t + 2.75, "near", off)]
        order += [(t + 2.7, "c", off), (t + 5.2, "p", off), (t + 5.3, "far", off)]
    return [event[1:] for event in sorted(order, key=lambda event: event[0])]


def goes_on(H, dist, way, part):
    return dist + 1 < H or (dist + 1 == H and part == way)


def kernel(
    Y, Z, tokens,
    acts_hbm, outg_hbm, inp_hbm, outp_hbm, len_hbm, q_hbm,
    out_ref,
    acts, outg, inp, outp, lens, qraw, stage, gath, halves, other, both, spare, lives, qall, tok, part, total, ar1, ar2, ar3, mine, gsc, sco, ret,
    loc_sem, act_loc, act_send, act_recv, og_sem, z_send, z_recv, r_send, r_recv, y_send, y_recv, cx_send, cx_recv,
    pt_send, pt_recv, sw_sem,
    t_send, t_recv, q_send, q_recv, a_send, a_recv,
):
    H = Z // 2
    dpi, qi = lax.axis_index("dp"), lax.axis_index("query")
    y, xl = dpi // 2, dpi % 2
    xh, z, c = qi // (2 * Z), (qi // 2) % Z, qi % 2

    def at(y_, xl_, xh_, z_, c_):
        return (y_ * 2 + xl_, xh_ * (2 * Z) + z_ * 2 + c_)

    def zp(off):
        return (z + (off + Z)) % Z

    def z_peer(off):
        return at(y, xl, xh, zp(off), c)

    def y_peer(off):
        return at((y + off) % Y, xl, xh, z, c)

    def x_peer(m):
        return at(y, (xl + (m // 2) % 2) % 2, (xh + m // 4) % 2, z, (c + m % 2) % 2)

    cross = at(y, 1 - xl, 1 - xh, z, c)
    partner = at(y, 1 - xl, xh, z, c)
    sibling = at(y, xl, xh, z, 1 - c)

    pending = []

    def push(ref_src, ref_dst, send, recv, to):
        copy = pltpu.make_async_remote_copy(
            src_ref=ref_src, dst_ref=ref_dst, send_sem=send, recv_sem=recv, device_id=to, device_id_type=MESH
        )
        copy.start()
        pending.append(copy)

    def got(ref, sem):
        pltpu.make_async_copy(ref, ref, sem).wait()

    loads = [
        pltpu.make_async_copy(inp_hbm, inp, loc_sem.at[0]),
        pltpu.make_async_copy(outp_hbm, outp, loc_sem.at[1]),
        pltpu.make_async_copy(q_hbm, qraw, loc_sem.at[2]),
        pltpu.make_async_copy(len_hbm, lens, loc_sem.at[3]),
    ]
    for load in loads:
        load.start()

    barrier = pltpu.get_barrier_semaphore()
    peers = [y_peer(d) for d in range(1, Y)] + [z_peer(d) for d in range(1, Z)] + [x_peer(m) for m in range(7, 0, -1)]
    for peer in peers:
        pl.semaphore_signal(barrier, inc=1, device_id=peer, device_id_type=MESH)

    order = gather_order(Z)
    folds = [event for event in order if event[0] in ("near", "far")]

    def window(name, off):
        return (xh if name == "near" else 1 - xh) * Z + zp(off)

    def act_columns(k, cc):
        return pl.ds(pl.multiple_of(k * (2 * IN_COLS) + cc * (IN_COLS - RANK), 128), IN_PAD)

    def act_slot(k, cc):
        return acts.at[pl.ds(pl.multiple_of(cc * TOK, TOK), TOK), pl.ds(pl.multiple_of(k * IN_PAD, IN_PAD), IN_PAD)]

    def out_slot(cc):
        return outg.at[pl.ds(pl.multiple_of(cc * TOK, TOK), TOK), :]

    mate = at(y + 1 - 2 * (y % 2), xl, xh, z, c)
    side = (y + xl) % 2

    def piece(h, off, p):
        return gath.at[pl.ds(pl.multiple_of((h * Z + zp(off)) * (2 * PIECE) + p * PIECE, 16), PIECE), :]

    def quarter(off, r):
        first = (xh * Z + zp(off)) * (2 * PIECE) + side * PIECE + r * 80
        return gath.at[pl.ds(pl.multiple_of(first, 16), PIECE - 80 if r else 80), :]

    stage[...] = jnp.zeros_like(stage)
    loads[0].wait()
    loads[1].wait()
    stage[:, 0:IN_COLS] = inp[...].astype(jnp.float32)
    plain = stage[...]
    shifted = pltpu.roll(plain, IN_PAD - RANK, 1)
    full = jnp.where(c == 1, shifted[:, 0:FULL], plain[:, 0:FULL])
    tile = jnp.where(c == 1, plain[:, 0:128], plain[:, FULL:IN_PAD])
    lane16 = lax.broadcasted_iota(jnp.int32, (HALF // 2, TOK), 1)

    def block_rows(k, p, first, count):
        return pl.ds(pl.multiple_of(k * (2 * PIECE) + p * PIECE + first, 16), count)

    for p in range(2):
        for j in range(3):
            chunk = full[p * HALF : (p + 1) * HALF, 128 * j : 128 * j + 128]
            gath[block_rows(xh * Z + z, p, j * HALF, HALF), :] = chunk.astype(jnp.bfloat16)
        gath[block_rows(xh * Z + z, p, 3 * HALF, HALF), :] = outp[p * HALF : (p + 1) * HALF, :]
        upper, lower = tile[p * HALF : p * HALF + 16], tile[p * HALF + 16 : (p + 1) * HALF]
        folded = jnp.where(lane16 < RANK, upper, pltpu.roll(lower, RANK, 1))
        gath[block_rows(xh * Z + z, p, 4 * HALF, HALF // 2), :] = folded.astype(jnp.bfloat16)
    pl.semaphore_wait(barrier, len(peers))

    lane_q = lax.broadcasted_iota(jnp.int32, (Q_ROWS, TOK), 1)
    q_cols = qraw.shape[1]

    def q_slot(h, cc):
        return (h * 2 + cc) * Q_ROWS

    def q_piece(h, cc, p):
        half = Q_ROWS // 2
        return qall.at[pl.ds(pl.multiple_of(q_slot(h, cc) + p * half, half), half), :]

    own_q = pl.ds(pl.multiple_of(q_slot(xh, c), Q_ROWS), Q_ROWS)

    def pair_queries():
        loads[2].wait()
        for m in range(q_cols // 256):
            first = qraw[:, 128 * m : 128 * m + 128].astype(jnp.float32)
            second = qraw[:, q_cols // 2 + 128 * m : q_cols // 2 + 128 * m + 128].astype(jnp.float32)
            low = jnp.where(lane_q < RANK, first, pltpu.roll(second, RANK, 1))
            high = jnp.where(lane_q < RANK, pltpu.roll(first, RANK, 1), second)
            qall[own_q, 256 * m : 256 * m + 128] = low.astype(jnp.bfloat16)
            qall[own_q, 256 * m + 128 : 256 * m + 256] = high.astype(jnp.bfloat16)

    sums = [jnp.zeros((RANK, 2 * TOK), jnp.float32), jnp.zeros((RANK, 2 * TOK), jnp.float32)]
    ref = piece(xh, 0, side)
    for d in range(H - 1, 0, -1):
        for sign in (1, -1):
            push(ref, ref, z_send.at[H - 1 + sign * d], z_recv.at[H - 1 - sign * d], z_peer(sign * d))
    push(ref, ref, cx_send.at[H - 1], cx_recv.at[H - 1], cross)
    own_loads = []
    for j, fold in enumerate(folds):
        k = window(*fold)
        own_loads.append(pltpu.make_async_copy(acts_hbm.at[:, act_columns(k, c)], act_slot(k, c), act_loc.at[j]))
        own_loads[-1].start()
        if j == 0:
            out_load = pltpu.make_async_copy(outg_hbm, out_slot(c), og_sem.at[0])
            out_load.start()
    for event in order:
        kind, off = event
        slot = H - 1 + off
        if kind == "z":
            ref = piece(xh, off, side)
            if off == H:
                got(quarter(H, 0), r_recv.at[0])
                got(quarter(H, 1), r_recv.at[1])
            else:
                got(ref, z_recv.at[slot])
            for r, sign in ((0, 1), (1, -1)):
                if off == -sign * (H - 1):
                    relay = quarter(off, r)
                    push(relay, relay, r_send.at[r], r_recv.at[r], z_peer(sign))
            push(ref, ref, cx_send.at[slot], cx_recv.at[slot], cross)
            push(ref, ref, y_send.at[slot], y_recv.at[slot], mate)
        elif kind == "y":
            got(piece(xh, off, 1 - side), y_recv.at[slot])
        elif kind == "c":
            ref = piece(1 - xh, off, 1 - side)
            got(ref, cx_recv.at[slot])
            push(ref, ref, pt_send.at[slot], pt_recv.at[slot], partner)
        elif kind == "p":
            got(piece(1 - xh, off, side), pt_recv.at[slot])
        elif event == ("q", 0):
            ref = q_piece(1 - xh, c, 1 - xl)
            got(ref, q_recv.at[0])
            push(ref, ref, q_send.at[2], q_recv.at[2], partner)
            push(ref, ref, q_send.at[3], q_recv.at[3], sibling)
        elif event == ("q", 1):
            ref = q_piece(1 - xh, c, xl)
            got(ref, q_recv.at[2])
            push(ref, ref, q_send.at[4], q_recv.at[4], sibling)
        else:
            j = folds.index(event)
            if j == 0:
                for i, fold in enumerate(folds):
                    k = window(*fold)
                    push(acts_hbm.at[:, act_columns(k, 1 - c)], act_slot(k, c), act_send.at[i], act_recv.at[i], sibling)
                    if i == 0:
                        push(outg_hbm, out_slot(c), og_sem.at[1], og_sem.at[2], sibling)
                pair_queries()
                ref = q_piece(xh, c, xl)
                push(ref, ref, q_send.at[0], q_recv.at[0], cross)
                ref = qall.at[own_q, :]
                push(ref, ref, q_send.at[1], q_recv.at[1], sibling)
                lane1 = lax.broadcasted_iota(jnp.int32, (8, TOK), 1)
                counts = jnp.zeros((8, TOK), jnp.int32)
                loads[3].wait()
                for e in range(TOK // SEQ):
                    counts = jnp.where(lane1 // SEQ == e, lens[e], counts)
                lives[c] = (lane1 % SEQ < counts).astype(jnp.float32)
                push(lives.at[c], lives.at[c], sw_sem.at[2], sw_sem.at[3], sibling)
                out_load.wait()
                got(out_slot(1 - c), og_sem.at[2])
            k = window(*event)
            own_loads[j].wait()
            got(act_slot(k, 1 - c), act_recv.at[j])
            weights = [
                jnp.concatenate([gath[block_rows(k, p, j * HALF, HALF), :] for p in range(2)], axis=0) for j in range(4)
            ]
            last = []
            for p in range(2):
                folded = gath[block_rows(k, p, 4 * HALF, HALF // 2), :].astype(jnp.float32)
                turned = pltpu.roll(folded, RANK, 1)
                for straight in (0, 1):
                    last.append(jnp.where(lane16 // RANK == c, jnp.where(c == straight, folded, turned), 0.0))
            last = jnp.concatenate(last, axis=0).astype(jnp.bfloat16)
            whole = acts[:, pl.ds(pl.multiple_of(k * IN_PAD + c * 128, 128), FULL)]
            tile = acts[:, pl.ds(pl.multiple_of(k * IN_PAD + (1 - c) * FULL, 128), 128)]
            weight = jnp.concatenate(weights[0:3] + [last], axis=1)
            sums[0] = sums[0] + dot(weight, jnp.concatenate([whole, tile], axis=1), NT)
            columns = pl.ds(pl.multiple_of(k * (2 * OUT_COLS) + c * OUT_COLS, OUT_COLS), OUT_COLS)
            sums[1] = sums[1] + dot(weights[3], outg[:, columns], NT)

    halves[0] = sums[0]
    halves[1] = sums[1]
    push(halves.at[1 - c], other, sw_sem.at[0], sw_sem.at[1], sibling)
    got(lives.at[1 - c], sw_sem.at[3])
    live = jnp.concatenate([lives[0, 0:1, :], lives[1, 0:1, :]], axis=1)
    got(other, sw_sem.at[1])
    masked = (halves[c] + other[...]) * live
    both[...] = masked
    hi, lo = split(masked)
    hi_lo = jnp.concatenate([hi, lo], axis=1)
    twice = jnp.concatenate([hi_lo, hi_lo], axis=0)
    lo_hi = jnp.concatenate([lo, hi], axis=1)
    gram = dot(hi_lo, twice, NT) + dot(lo_hi, twice, NT)
    half = RANK // 2
    lane = lax.broadcasted_iota(jnp.int32, (half, TOK), 1)
    part[...] = jnp.where(lane < RANK, gram[0:half], gram[half:])

    rows_x = half // 4

    def x_rows(m):
        index = ((xh + m // 4) % 2) * 2 + (xl + (m // 2) % 2) % 2
        return pl.ds(pl.multiple_of(index * rows_x, rows_x), rows_x)

    def tok_piece(zz, p):
        return tok.at[pl.ds(pl.multiple_of(zz * TOK + p * RANK, RANK), RANK), :]

    def tok_step(dist):
        for way, sign in ((0, -1), (1, 1)):
            for p in (0, 1):
                ref = tok_piece(zp(sign * dist), p)
                if dist == H and p != way:
                    continue
                if dist > 0:
                    got(ref, t_recv.at[way, dist - 1, p])
                if goes_on(H, dist, way, p):
                    push(ref, ref, t_send.at[way, dist, p], t_recv.at[way, dist, p], z_peer(-sign))

    for j, m in enumerate((4, 6, 2)):
        push(part.at[x_rows(m), :], ar1.at[j], a_send.at[0, j], a_recv.at[0], x_peer(m))
    for cc in range(2):

        @pl.when(c == cc)
        def _():
            tok[pl.ds(pl.multiple_of(z * TOK + cc * RANK, RANK), RANK), :] = both[:, cc * TOK : (cc + 1) * TOK]
            spare[...] = both[:, (1 - cc) * TOK : (2 - cc) * TOK]

    push(spare, tok_piece(z, c), sw_sem.at[4], sw_sem.at[5], sibling)
    got(ar1, a_recv.at[0])
    summed = part[x_rows(0), :]
    for j in range(3):
        summed = summed + ar1[j]
    mine[0] = summed
    for d in range(1, Z):
        push(mine.at[0], ar2.at[d - 1], a_send.at[1, d - 1], a_recv.at[1], z_peer(d))
    got(tok_piece(z, 1 - c), sw_sem.at[5])
    tok_step(0)
    tok_step(1)
    got(ar2, a_recv.at[1])
    for d in range(Z - 1):
        summed = summed + ar2[d]
    mine[1] = summed
    for d in range(1, Y):
        push(mine.at[1], ar3.at[d - 1], a_send.at[2, d - 1], a_recv.at[2], y_peer(d))
    if H > 2:
        tok_step(2)
    got(ar3, a_recv.at[2])
    for d in range(Y - 1):
        summed = summed + ar3[d]

    def total_rows(cc):
        return total.at[pl.ds(pl.multiple_of((cc * 4 + xh * 2 + xl) * rows_x, rows_x), rows_x), :]

    here = total_rows(c)
    here[...] = summed
    for m in (5, 7, 4, 6, 3, 2, 1):
        push(here, here, a_send.at[3, m - 1], a_recv.at[3], x_peer(m))
    if H > 3:
        tok_step(3)
    got(total.at[0 : RANK - rows_x, :], a_recv.at[3])
    if H > 1:
        tok_step(H)

    ins, outs = total[0:half], total[half:]
    sides = jnp.concatenate(
        [
            jnp.where(lane < RANK, ins, pltpu.roll(outs, RANK, 1)),
            jnp.where(lane < RANK, pltpu.roll(ins, RANK, 1), outs),
        ],
        axis=0,
    )
    inverses = damped_inverses(sides, tokens)
    lane = lax.broadcasted_iota(jnp.int32, (RANK, TOK), 1)
    blocks = jnp.concatenate(
        [jnp.where(lane < RANK, inverses, 0.0), jnp.where(lane < RANK, 0.0, inverses)], axis=0
    )
    hi, lo = split(blocks)
    blocks = jnp.concatenate([hi, lo, hi], axis=1)
    example = lax.broadcasted_iota(jnp.int32, (SEQ // 2, TOK), 0)
    token = lax.broadcasted_iota(jnp.int32, (SEQ // 2, TOK), 1)
    belongs = (token // SEQ == example).astype(jnp.float32)
    nothing = jnp.zeros((RANK, TOK), jnp.bfloat16)
    for k in range(Z):
        if k % 2 == 0:
            rows = [split(tok[(k + i) * TOK : (k + i + 1) * TOK, :]) for i in range(2)]
            hi = jnp.concatenate([rows[0][0], rows[1][0]], axis=1)
            lo = jnp.concatenate([rows[0][1], rows[1][1]], axis=1)
            pair = dot(blocks, jnp.concatenate([hi, hi, lo], axis=0))
        ins, outs = pair[0:RANK, (k % 2) * TOK : (k % 2 + 1) * TOK], pair[RANK:, (k % 2) * TOK : (k % 2 + 1) * TOK]
        left, right = [], []
        for w in split(outs):
            spread = (w.astype(jnp.float32)[:, None, :] * belongs[None, :, :]).astype(jnp.bfloat16)
            spread = spread.reshape(RANK * 8, TOK)
            left.append(jnp.concatenate([spread[0 : half * 8], spread[half * 8 :]], axis=1))
        for w in split(ins):
            right += [jnp.concatenate([w, nothing], axis=1), jnp.concatenate([nothing, w], axis=1)]
        grads = dot(left[0], jnp.concatenate(right, axis=0), NT)
        grads = grads[:, 0:TOK] + (grads[:, TOK:] + dot(left[1], jnp.concatenate(right[0:2], axis=0), NT))
        gsc[:, k * 8 : (k + 1) * 8, :] = grads.reshape(half, 8, TOK)

    got(qall.at[pl.ds(pl.multiple_of(q_slot(xh, 1 - c), Q_ROWS), Q_ROWS), :], q_recv.at[1])
    got(q_piece(1 - xh, 1 - c, 1 - xl), q_recv.at[3])
    got(q_piece(1 - xh, 1 - c, xl), q_recv.at[4])
    scores = jnp.zeros((2 * 8 * Z, TOK), jnp.float32)
    for m in range(half // 2):
        both = jnp.concatenate([gsc[2 * m], gsc[2 * m + 1]], axis=1)
        hi, lo = split(both)
        scores = scores + dot(jnp.concatenate([hi, lo], axis=0), qall[:, 256 * m : 256 * m + 256], NT)
    sco[...] = scores[0 : 8 * Z] + scores[8 * Z :]
    for d in range(1, Z):
        push(
            sco.at[pl.ds(pl.multiple_of(zp(d) * 8, 8), 8), :], ret.at[d], a_send.at[4, d - 1], a_recv.at[4], z_peer(d)
        )
    ret[0] = sco[pl.ds(pl.multiple_of(z * 8, 8), 8), :]
    got(ret.at[1:Z], a_recv.at[4])
    lane8 = lax.broadcasted_iota(jnp.int32, (8, TOK), 1)
    width = Z * RANK
    for m in range(Z // 2):
        first = ret[zp(-2 * m)]
        second = ret[zp(-2 * m - 1)]
        out_ref[:, 128 * m : 128 * m + 128] = jnp.where(lane8 < RANK, first, pltpu.roll(second, RANK, 1))
        out_ref[:, width + 128 * m : width + 128 * m + 128] = jnp.where(
            lane8 < RANK, pltpu.roll(first, RANK, 1), second
        )
    for copy in pending:
        copy.wait_send()


def solution(mesh):
    Y, Z = mesh.shape["dp"] // 2, mesh.shape["query"] // 4
    H = Z // 2

    def on_device(activations, out_grads, in_projection, out_projection, lengths, queries):
        tokens = activations.shape[0] * mesh.shape["dp"] * mesh.shape["query"]
        f32, bf16 = jnp.float32, jnp.bfloat16
        sem = pltpu.SemaphoreType.DMA
        return pl.pallas_call(
            functools.partial(kernel, Y, Z, tokens),
            out_shape=pltpu.VMEM((lengths.shape[0], Z * 4 * Q_ROWS), f32),
            in_specs=[pl.BlockSpec(memory_space=pltpu.HBM)] * 6,
            out_specs=pl.BlockSpec(memory_space=pltpu.VMEM),
            scratch_shapes=[
                pltpu.VMEM((2 * TOK, 2 * Z * IN_PAD), bf16),
                pltpu.VMEM((2 * TOK, out_grads.shape[1]), bf16),
                pltpu.VMEM(in_projection.shape, bf16),
                pltpu.VMEM(out_projection.shape, bf16),
                pltpu.SMEM(lengths.shape, jnp.int32),
                pltpu.VMEM(queries.shape, bf16),
                pltpu.VMEM((RANK, IN_PAD), f32),
                pltpu.VMEM((4 * Z * PIECE, TOK), bf16),
                pltpu.VMEM((2, RANK, 2 * TOK), f32),
                pltpu.VMEM((RANK, 2 * TOK), f32),
                pltpu.VMEM((RANK, 2 * TOK), f32),
                pltpu.VMEM((RANK, TOK), f32),
                pltpu.VMEM((2, 8, TOK), f32),
                pltpu.VMEM((4 * Q_ROWS, queries.shape[1]), bf16),
                pltpu.VMEM((Z * TOK, TOK), f32),
                pltpu.VMEM((RANK // 2, TOK), f32),
                pltpu.VMEM((RANK, TOK), f32),
                pltpu.VMEM((3, RANK // 8, TOK), f32),
                pltpu.VMEM((Z - 1, RANK // 8, TOK), f32),
                pltpu.VMEM((Y - 1, RANK // 8, TOK), f32),
                pltpu.VMEM((2, RANK // 8, TOK), f32),
                pltpu.VMEM((RANK // 2, 8 * Z, TOK), f32),
                pltpu.VMEM((8 * Z, TOK), f32),
                pltpu.VMEM((Z, 8, TOK), f32),
                sem((4,)),
                sem((2 * Z,)),
                sem((2 * Z,)),
                sem((2 * Z,)),
                sem((3,)),
                sem((Z,)),
                sem((Z,)),
                sem((2,)),
                sem((2,)),
                sem((Z,)),
                sem((Z,)),
                sem((Z,)),
                sem((Z,)),
                sem((Z,)),
                sem((Z,)),
                sem((6,)),
                sem((2, H, 2)),
                sem((2, H, 2)),
                sem((5,)),
                sem((5,)),
                sem((5, 7)),
                sem((5,)),
            ],
            compiler_params=pltpu.CompilerParams(
                collective_id=0, has_side_effects=True, vmem_limit_bytes=60 * 1024 * 1024
            ),
        )(activations, out_grads, in_projection, out_projection, lengths, queries)

    placed = (
        P(("dp", "query"), None),
        P(("dp", "query"), None),
        P(None, "query"),
        P(None, "query"),
        P(("dp", "query")),
        P("query", None),
    )
    return jax.shard_map(
        on_device, mesh=mesh, in_specs=placed, out_specs=P(("dp", "query"), None), check_vma=False
    )
```

```python
import functools

import jax
import jax.numpy as jnp
from jax import lax
from jax.experimental import pallas as pl
from jax.experimental.pallas import tpu as pltpu
from jax.sharding import PartitionSpec as P

MESH = pl.DeviceIdType.MESH
RANK = 64
SEQ = 16
TOK = 128
IN_COLS = 448
IN_PAD = 512
OUT_COLS = 128
FULL = 384
HALF = RANK // 2
PIECE = 4 * HALF + HALF // 2
Q_ROWS = 32
NT = (((1,), (1,)), ((), ()))
NN = (((1,), (0,)), ((), ()))


def dot(a, b, dims=NN):
    return lax.dot_general(a, b, dims, preferred_element_type=jnp.float32)


def split(x):
    hi = x.astype(jnp.bfloat16)
    return hi, (x - hi.astype(jnp.float32)).astype(jnp.bfloat16)


def inverse_of_four(p):
    a, b, d = p[0][0], p[0][1], p[1][1]
    scale = 1.0 / (a * d - b * b)
    u00, u01, u11 = d * scale, -b * scale, a * scale
    c = [[p[0][2], p[0][3]], [p[1][2], p[1][3]]]
    x = [[u00 * c[0][j] + u01 * c[1][j] for j in range(2)], [u01 * c[0][j] + u11 * c[1][j] for j in range(2)]]
    s00 = p[2][2] - (c[0][0] * x[0][0] + c[1][0] * x[1][0])
    s01 = p[2][3] - (c[0][0] * x[0][1] + c[1][0] * x[1][1])
    s11 = p[3][3] - (c[0][1] * x[0][1] + c[1][1] * x[1][1])
    scale = 1.0 / (s00 * s11 - s01 * s01)
    t00, t01, t11 = s11 * scale, -s01 * scale, s00 * scale
    w = [[x[i][0] * t00 + x[i][1] * t01, x[i][0] * t01 + x[i][1] * t11] for i in range(2)]
    v00 = u00 + w[0][0] * x[0][0] + w[0][1] * x[0][1]
    v01 = u01 + w[0][0] * x[1][0] + w[0][1] * x[1][1]
    v11 = u11 + w[1][0] * x[1][0] + w[1][1] * x[1][1]
    return [
        [v00, v01, -w[0][0], -w[0][1]],
        [v01, v11, -w[1][0], -w[1][1]],
        [-w[0][0], -w[1][0], t00, t01],
        [-w[0][1], -w[1][1], t01, t11],
    ]


def damped_inverses(total, tokens):
    lane = lax.broadcasted_iota(jnp.int32, (RANK, TOK), 1)
    row = lax.broadcasted_iota(jnp.int32, (RANK, TOK), 0)
    column = lane % RANK
    left = lane < RANK
    work = total * (1.0 / tokens)
    diagonal = jnp.where(column == row, work, 0.0)
    trace = jnp.where(left, jnp.sum(jnp.where(left, diagonal, 0.0)), jnp.sum(jnp.where(left, 0.0, diagonal)))
    work = jnp.where(column == row, work + 0.1 * trace / RANK, work)
    first = jnp.where(left, 0, RANK)
    column1 = lax.broadcasted_iota(jnp.int32, (1, TOK), 1) % RANK
    for k in range(0, RANK, 4):
        columns = [jnp.take_along_axis(work, first + (k + i), axis=1) for i in range(4)]
        rows = [work[k + i : k + i + 1] for i in range(4)]
        pivot = inverse_of_four([[columns[j][k + i : k + i + 1] for j in range(4)] for i in range(4)])
        scaled = []
        for i in range(4):
            value = (pivot[i][0] * rows[0] + pivot[i][1] * rows[1]) + (pivot[i][2] * rows[2] + pivot[i][3] * rows[3])
            for j in range(4):
                value = jnp.where(column1 == k + j, pivot[i][j], value)
            scaled.append(value)
        work = jnp.where((column >= k) & (column < k + 4), 0.0, work)
        work = (work - columns[0] * scaled[0] - columns[1] * scaled[1]) - (
            columns[2] * scaled[2] + columns[3] * scaled[3]
        )
        for i in range(4):
            work = jnp.where(row == k + i, scaled[i], work)
    return work


def gather_order(Z):
    H = Z // 2
    times = {d: 4.5 + 0.95 * (H - 1 - d) for d in range(1, H)}
    times[H] = max(times.get(H - 1, 4.5) + 2.5, 7.0)
    order = [(0.3, "near", 0), (5.0, "q", 0), (9.4, "q", 1)]
    for off in [0] + [sign * d for d in range(H - 1, 0, -1) for sign in (-1, 1)] + [H]:
        t = times[abs(off)] if off else 0.0
        if off:
            order += [(t, "z", off), (t + 2.7, "y", off), (t + 2.75, "near", off)]
        order += [(t + 2.7, "c", off), (t + 5.2, "p", off), (t + 5.3, "far", off)]
    return [event[1:] for event in sorted(order, key=lambda event: event[0])]


def far_first(count):
    half = count // 2
    return [half] + [sign * d for d in range(half - 1, 0, -1) for sign in (1, -1)] + [0]


def goes_on(H, dist, way, part):
    return dist + 1 < H or (dist + 1 == H and part == way)


def kernel(
    Y, Z, tokens,
    acts_hbm, outg_hbm, inp_hbm, outp_hbm, len_hbm, q_hbm,
    out_ref,
    acts, outg, inp, outp, lens, qraw, stage, gath, halves, other, both, spare, lives, qall, tok, part, total, ar1, ar2, ar3, mine, gsc, sco, ret,
    loc_sem, act_loc, act_send, act_recv, og_sem, z_send, z_recv, r_send, r_recv, y_send, y_recv, cx_send, cx_recv,
    pt_send, pt_recv, sw_sem,
    t_send, t_recv, q_send, q_recv, a_send, a_recv,
):
    H = Z // 2
    dpi, qi = lax.axis_index("dp"), lax.axis_index("query")
    y, xl = dpi // 2, dpi % 2
    xh, z, c = qi // (2 * Z), (qi // 2) % Z, qi % 2

    def at(y_, xl_, xh_, z_, c_):
        return (y_ * 2 + xl_, xh_ * (2 * Z) + z_ * 2 + c_)

    def zp(off):
        return (z + (off + Z)) % Z

    def z_peer(off):
        return at(y, xl, xh, zp(off), c)

    def y_peer(off):
        return at((y + off) % Y, xl, xh, z, c)

    def x_peer(m):
        return at(y, (xl + (m // 2) % 2) % 2, (xh + m // 4) % 2, z, (c + m % 2) % 2)

    cross = at(y, 1 - xl, 1 - xh, z, c)
    partner = at(y, 1 - xl, xh, z, c)
    sibling = at(y, xl, xh, z, 1 - c)

    pending = []

    def push(ref_src, ref_dst, send, recv, to):
        copy = pltpu.make_async_remote_copy(
            src_ref=ref_src, dst_ref=ref_dst, send_sem=send, recv_sem=recv, device_id=to, device_id_type=MESH
        )
        copy.start()
        pending.append(copy)

    def got(ref, sem):
        pltpu.make_async_copy(ref, ref, sem).wait()

    def settle(keep):
        while len(pending) > keep:
            pending.pop(0).wait_send()

    loads = [
        pltpu.make_async_copy(inp_hbm, inp, loc_sem.at[0]),
        pltpu.make_async_copy(outp_hbm, outp, loc_sem.at[1]),
        pltpu.make_async_copy(q_hbm, qraw, loc_sem.at[2]),
        pltpu.make_async_copy(len_hbm, lens, loc_sem.at[3]),
    ]
    for load in loads:
        load.start()

    barrier = pltpu.get_barrier_semaphore()
    peers = [y_peer(d) for d in range(1, Y)] + [z_peer(d) for d in range(1, Z)] + [x_peer(m) for m in range(7, 0, -1)]
    for peer in peers:
        pl.semaphore_signal(barrier, inc=1, device_id=peer, device_id_type=MESH)

    order = gather_order(Z)
    folds = [event for event in order if event[0] in ("near", "far")]

    def window(name, off):
        return (xh if name == "near" else 1 - xh) * Z + zp(off)

    def act_columns(k, cc):
        return pl.ds(pl.multiple_of(k * (2 * IN_COLS) + cc * (IN_COLS - RANK), 128), IN_PAD)

    def act_slot(k, cc):
        return acts.at[pl.ds(pl.multiple_of(cc * TOK, TOK), TOK), pl.ds(pl.multiple_of(k * IN_PAD, IN_PAD), IN_PAD)]

    def out_slot(cc):
        return outg.at[pl.ds(pl.multiple_of(cc * TOK, TOK), TOK), :]

    mate = at(y + 1 - 2 * (y % 2), xl, xh, z, c)
    side = (y + xl) % 2

    def piece(h, off, p):
        return gath.at[pl.ds(pl.multiple_of((h * Z + zp(off)) * (2 * PIECE) + p * PIECE, 16), PIECE), :]

    def quarter(off, r):
        first = (xh * Z + zp(off)) * (2 * PIECE) + side * PIECE + r * 80
        return gath.at[pl.ds(pl.multiple_of(first, 16), PIECE - 80 if r else 80), :]

    stage[...] = jnp.zeros_like(stage)
    loads[0].wait()
    loads[1].wait()
    stage[:, 0:IN_COLS] = inp[...].astype(jnp.float32)
    plain = stage[...]
    shifted = pltpu.roll(plain, IN_PAD - RANK, 1)
    full = jnp.where(c == 1, shifted[:, 0:FULL], plain[:, 0:FULL])
    tile = jnp.where(c == 1, plain[:, 0:128], plain[:, FULL:IN_PAD])
    lane16 = lax.broadcasted_iota(jnp.int32, (HALF // 2, TOK), 1)

    def block_rows(k, p, first, count):
        return pl.ds(pl.multiple_of(k * (2 * PIECE) + p * PIECE + first, 16), count)

    for p in range(2):
        for j in range(3):
            chunk = full[p * HALF : (p + 1) * HALF, 128 * j : 128 * j + 128]
            gath[block_rows(xh * Z + z, p, j * HALF, HALF), :] = chunk.astype(jnp.bfloat16)
        gath[block_rows(xh * Z + z, p, 3 * HALF, HALF), :] = outp[p * HALF : (p + 1) * HALF, :]
        upper, lower = tile[p * HALF : p * HALF + 16], tile[p * HALF + 16 : (p + 1) * HALF]
        folded = jnp.where(lane16 < RANK, upper, pltpu.roll(lower, RANK, 1))
        gath[block_rows(xh * Z + z, p, 4 * HALF, HALF // 2), :] = folded.astype(jnp.bfloat16)
    pl.semaphore_wait(barrier, len(peers))

    lane_q = lax.broadcasted_iota(jnp.int32, (Q_ROWS, TOK), 1)
    q_cols = qraw.shape[1]

    def q_slot(h, cc):
        return (h * 2 + cc) * Q_ROWS

    def q_piece(h, cc, p):
        half = Q_ROWS // 2
        return qall.at[pl.ds(pl.multiple_of(q_slot(h, cc) + p * half, half), half), :]

    own_q = pl.ds(pl.multiple_of(q_slot(xh, c), Q_ROWS), Q_ROWS)

    def pair_queries():
        loads[2].wait()
        for m in range(q_cols // 256):
            first = qraw[:, 128 * m : 128 * m + 128].astype(jnp.float32)
            second = qraw[:, q_cols // 2 + 128 * m : q_cols // 2 + 128 * m + 128].astype(jnp.float32)
            low = jnp.where(lane_q < RANK, first, pltpu.roll(second, RANK, 1))
            high = jnp.where(lane_q < RANK, pltpu.roll(first, RANK, 1), second)
            qall[own_q, 256 * m : 256 * m + 128] = low.astype(jnp.bfloat16)
            qall[own_q, 256 * m + 128 : 256 * m + 256] = high.astype(jnp.bfloat16)

    sums = [jnp.zeros((RANK, 2 * TOK), jnp.float32), jnp.zeros((RANK, 2 * TOK), jnp.float32)]
    ref = piece(xh, 0, side)
    for d in range(H - 1, 0, -1):
        for sign in (1, -1):
            push(ref, ref, z_send.at[H - 1 + sign * d], z_recv.at[H - 1 - sign * d], z_peer(sign * d))
    push(ref, ref, cx_send.at[H - 1], cx_recv.at[H - 1], cross)
    own_loads = []
    for j, fold in enumerate(folds):
        k = window(*fold)
        own_loads.append(pltpu.make_async_copy(acts_hbm.at[:, act_columns(k, c)], act_slot(k, c), act_loc.at[j]))
        own_loads[-1].start()
        if j == 0:
            out_load = pltpu.make_async_copy(outg_hbm, out_slot(c), og_sem.at[0])
            out_load.start()
    for event in order:
        kind, off = event
        slot = H - 1 + off
        if kind == "z":
            ref = piece(xh, off, side)
            if off == H:
                got(quarter(H, 0), r_recv.at[0])
                got(quarter(H, 1), r_recv.at[1])
            else:
                got(ref, z_recv.at[slot])
            for r, sign in ((0, 1), (1, -1)):
                if off == -sign * (H - 1):
                    relay = quarter(off, r)
                    push(relay, relay, r_send.at[r], r_recv.at[r], z_peer(sign))
            push(ref, ref, cx_send.at[slot], cx_recv.at[slot], cross)
            push(ref, ref, y_send.at[slot], y_recv.at[slot], mate)
        elif kind == "y":
            got(piece(xh, off, 1 - side), y_recv.at[slot])
        elif kind == "c":
            ref = piece(1 - xh, off, 1 - side)
            got(ref, cx_recv.at[slot])
            push(ref, ref, pt_send.at[slot], pt_recv.at[slot], partner)
        elif kind == "p":
            got(piece(1 - xh, off, side), pt_recv.at[slot])
        elif event == ("q", 0):
            ref = q_piece(1 - xh, c, 1 - xl)
            got(ref, q_recv.at[0])
            push(ref, ref, q_send.at[2], q_recv.at[2], partner)
            push(ref, ref, q_send.at[3], q_recv.at[3], sibling)
        elif event == ("q", 1):
            ref = q_piece(1 - xh, c, xl)
            got(ref, q_recv.at[2])
            push(ref, ref, q_send.at[4], q_recv.at[4], sibling)
        else:
            j = folds.index(event)
            if j == 0:
                for i, fold in enumerate(folds):
                    k = window(*fold)
                    push(acts_hbm.at[:, act_columns(k, 1 - c)], act_slot(k, c), act_send.at[i], act_recv.at[i], sibling)
                    if i == 0:
                        push(outg_hbm, out_slot(c), og_sem.at[1], og_sem.at[2], sibling)
                pair_queries()
                ref = q_piece(xh, c, xl)
                push(ref, ref, q_send.at[0], q_recv.at[0], cross)
                ref = qall.at[own_q, :]
                push(ref, ref, q_send.at[1], q_recv.at[1], sibling)
                lane1 = lax.broadcasted_iota(jnp.int32, (8, TOK), 1)
                counts = jnp.zeros((8, TOK), jnp.int32)
                loads[3].wait()
                for e in range(TOK // SEQ):
                    counts = jnp.where(lane1 // SEQ == e, lens[e], counts)
                lives[c] = (lane1 % SEQ < counts).astype(jnp.float32)
                push(lives.at[c], lives.at[c], sw_sem.at[2], sw_sem.at[3], sibling)
                out_load.wait()
                got(out_slot(1 - c), og_sem.at[2])
            k = window(*event)
            own_loads[j].wait()
            got(act_slot(k, 1 - c), act_recv.at[j])
            weights = [
                jnp.concatenate([gath[block_rows(k, p, j * HALF, HALF), :] for p in range(2)], axis=0) for j in range(4)
            ]
            last = []
            for p in range(2):
                folded = gath[block_rows(k, p, 4 * HALF, HALF // 2), :].astype(jnp.float32)
                turned = pltpu.roll(folded, RANK, 1)
                for straight in (0, 1):
                    last.append(jnp.where(lane16 // RANK == c, jnp.where(c == straight, folded, turned), 0.0))
            last = jnp.concatenate(last, axis=0).astype(jnp.bfloat16)
            whole = acts[:, pl.ds(pl.multiple_of(k * IN_PAD + c * 128, 128), FULL)]
            tile = acts[:, pl.ds(pl.multiple_of(k * IN_PAD + (1 - c) * FULL, 128), 128)]
            weight = jnp.concatenate(weights[0:3] + [last], axis=1)
            sums[0] = sums[0] + dot(weight, jnp.concatenate([whole, tile], axis=1), NT)
            columns = pl.ds(pl.multiple_of(k * (2 * OUT_COLS) + c * OUT_COLS, OUT_COLS), OUT_COLS)
            sums[1] = sums[1] + dot(weights[3], outg[:, columns], NT)

    halves[0] = sums[0]
    halves[1] = sums[1]
    push(halves.at[1 - c], other, sw_sem.at[0], sw_sem.at[1], sibling)
    got(lives.at[1 - c], sw_sem.at[3])
    live = jnp.concatenate([lives[0, 0:1, :], lives[1, 0:1, :]], axis=1)
    got(other, sw_sem.at[1])
    masked = (halves[c] + other[...]) * live
    both[...] = masked
    hi, lo = split(masked)
    hi_lo = jnp.concatenate([hi, lo], axis=1)
    twice = jnp.concatenate([hi_lo, hi_lo], axis=0)
    lo_hi = jnp.concatenate([lo, hi], axis=1)
    gram = dot(hi_lo, twice, NT) + dot(lo_hi, twice, NT)
    half = RANK // 2
    lane = lax.broadcasted_iota(jnp.int32, (half, TOK), 1)
    part[...] = jnp.where(lane < RANK, gram[0:half], gram[half:])

    rows_x = half // 4

    def x_rows(m):
        index = ((xh + m // 4) % 2) * 2 + (xl + (m // 2) % 2) % 2
        return pl.ds(pl.multiple_of(index * rows_x, rows_x), rows_x)

    def tok_piece(zz, p):
        return tok.at[pl.ds(pl.multiple_of(zz * TOK + p * RANK, RANK), RANK), :]

    def tok_step(dist):
        for way, sign in ((0, -1), (1, 1)):
            for p in (0, 1):
                ref = tok_piece(zp(sign * dist), p)
                if dist == H and p != way:
                    continue
                if dist > 0:
                    got(ref, t_recv.at[way, dist - 1, p])
                if goes_on(H, dist, way, p):
                    push(ref, ref, t_send.at[way, dist, p], t_recv.at[way, dist, p], z_peer(-sign))

    for j, m in enumerate((4, 6, 2)):
        push(part.at[x_rows(m), :], ar1.at[j], a_send.at[0, j], a_recv.at[0], x_peer(m))
    for cc in range(2):

        @pl.when(c == cc)
        def _():
            tok[pl.ds(pl.multiple_of(z * TOK + cc * RANK, RANK), RANK), :] = both[:, cc * TOK : (cc + 1) * TOK]
            spare[...] = both[:, (1 - cc) * TOK : (2 - cc) * TOK]

    push(spare, tok_piece(z, c), sw_sem.at[4], sw_sem.at[5], sibling)
    settle(30)
    got(ar1, a_recv.at[0])
    summed = part[x_rows(0), :]
    for j in range(3):
        summed = summed + ar1[j]
    mine[0] = summed
    for d in [off % Z for off in far_first(Z)[:-1]]:
        push(mine.at[0], ar2.at[d - 1], a_send.at[1, d - 1], a_recv.at[1], z_peer(d))
    got(tok_piece(z, 1 - c), sw_sem.at[5])
    tok_step(0)
    settle(25)
    tok_step(1)
    got(ar2, a_recv.at[1])
    for d in range(Z - 1):
        summed = summed + ar2[d]
    mine[1] = summed
    for d in [off % Y for off in far_first(Y)[:-1]]:
        push(mine.at[1], ar3.at[d - 1], a_send.at[2, d - 1], a_recv.at[2], y_peer(d))
    if H > 2:
        tok_step(2)
    settle(25)
    got(ar3, a_recv.at[2])
    for d in range(Y - 1):
        summed = summed + ar3[d]

    def total_rows(cc):
        return total.at[pl.ds(pl.multiple_of((cc * 4 + xh * 2 + xl) * rows_x, rows_x), rows_x), :]

    here = total_rows(c)
    here[...] = summed
    for m in (5, 7, 4, 6, 3, 2, 1):
        push(here, here, a_send.at[3, m - 1], a_recv.at[3], x_peer(m))
    if H > 3:
        tok_step(3)
    settle(15)
    got(total.at[0 : RANK - rows_x, :], a_recv.at[3])
    if H > 1:
        tok_step(H)

    ins, outs = total[0:half], total[half:]
    sides = jnp.concatenate(
        [
            jnp.where(lane < RANK, ins, pltpu.roll(outs, RANK, 1)),
            jnp.where(lane < RANK, pltpu.roll(ins, RANK, 1), outs),
        ],
        axis=0,
    )
    inverses = damped_inverses(sides, tokens)
    lane = lax.broadcasted_iota(jnp.int32, (RANK, TOK), 1)
    blocks = jnp.concatenate(
        [jnp.where(lane < RANK, inverses, 0.0), jnp.where(lane < RANK, 0.0, inverses)], axis=0
    )
    hi, lo = split(blocks)
    blocks = jnp.concatenate([hi, lo, hi], axis=1)
    example = lax.broadcasted_iota(jnp.int32, (SEQ // 2, TOK), 0)
    token = lax.broadcasted_iota(jnp.int32, (SEQ // 2, TOK), 1)
    belongs = (token // SEQ == example).astype(jnp.float32)
    nothing = jnp.zeros((RANK, TOK), jnp.bfloat16)
    got(qall.at[pl.ds(pl.multiple_of(q_slot(xh, 1 - c), Q_ROWS), Q_ROWS), :], q_recv.at[1])
    got(q_piece(1 - xh, 1 - c, 1 - xl), q_recv.at[3])
    got(q_piece(1 - xh, 1 - c, xl), q_recv.at[4])
    offs = far_first(Z)
    group = Z // 2
    for k in range(Z):
        if k % 2 == 0:
            rows = [
                split(tok[pl.ds(pl.multiple_of(zp(off) * TOK, TOK), TOK), :]) for off in offs[k : k + 2]
            ]
            hi = jnp.concatenate([rows[0][0], rows[1][0]], axis=1)
            lo = jnp.concatenate([rows[0][1], rows[1][1]], axis=1)
            pair = dot(blocks, jnp.concatenate([hi, hi, lo], axis=0))
        ins, outs = pair[0:RANK, (k % 2) * TOK : (k % 2 + 1) * TOK], pair[RANK:, (k % 2) * TOK : (k % 2 + 1) * TOK]
        left, right = [], []
        for w in split(outs):
            spread = (w.astype(jnp.float32)[:, None, :] * belongs[None, :, :]).astype(jnp.bfloat16)
            spread = spread.reshape(RANK * 8, TOK)
            left.append(jnp.concatenate([spread[0 : half * 8], spread[half * 8 :]], axis=1))
        for w in split(ins):
            right += [jnp.concatenate([w, nothing], axis=1), jnp.concatenate([nothing, w], axis=1)]
        grads = dot(left[0], jnp.concatenate(right, axis=0), NT)
        grads = grads[:, 0:TOK] + (grads[:, TOK:] + dot(left[1], jnp.concatenate(right[0:2], axis=0), NT))
        gsc[:, k * 8 : (k + 1) * 8, :] = grads.reshape(half, 8, TOK)
        if (k + 1) % group:
            continue
        first = k + 1 - group
        scores = jnp.zeros((2 * 8 * group, TOK), jnp.float32)
        for m in range(half // 2):
            mine_both = [gsc[2 * m + i, first * 8 : (k + 1) * 8, :] for i in range(2)]
            hi, lo = split(jnp.concatenate(mine_both, axis=1))
            scores = scores + dot(jnp.concatenate([hi, lo], axis=0), qall[:, 256 * m : 256 * m + 256], NT)
        sco[first * 8 : (k + 1) * 8, :] = scores[0 : 8 * group] + scores[8 * group :]
        for j in range(first, k + 1):
            if offs[j] == 0:
                ret[0] = sco[j * 8 : (j + 1) * 8, :]
            else:
                d = offs[j] % Z
                push(sco.at[j * 8 : (j + 1) * 8, :], ret.at[d], a_send.at[4, d - 1], a_recv.at[4], z_peer(d))
    settle(Z // 2 - 1)
    got(ret.at[1:Z], a_recv.at[4])
    lane8 = lax.broadcasted_iota(jnp.int32, (8, TOK), 1)
    width = Z * RANK
    for m in range(Z // 2):
        first = ret[zp(-2 * m)]
        second = ret[zp(-2 * m - 1)]
        out_ref[:, 128 * m : 128 * m + 128] = jnp.where(lane8 < RANK, first, pltpu.roll(second, RANK, 1))
        out_ref[:, width + 128 * m : width + 128 * m + 128] = jnp.where(
            lane8 < RANK, pltpu.roll(first, RANK, 1), second
        )
    settle(0)


def solution(mesh):
    Y, Z = mesh.shape["dp"] // 2, mesh.shape["query"] // 4
    H = Z // 2

    def on_device(activations, out_grads, in_projection, out_projection, lengths, queries):
        tokens = activations.shape[0] * mesh.shape["dp"] * mesh.shape["query"]
        f32, bf16 = jnp.float32, jnp.bfloat16
        sem = pltpu.SemaphoreType.DMA
        return pl.pallas_call(
            functools.partial(kernel, Y, Z, tokens),
            out_shape=pltpu.VMEM((lengths.shape[0], Z * 4 * Q_ROWS), f32),
            in_specs=[pl.BlockSpec(memory_space=pltpu.HBM)] * 6,
            out_specs=pl.BlockSpec(memory_space=pltpu.VMEM),
            scratch_shapes=[
                pltpu.VMEM((2 * TOK, 2 * Z * IN_PAD), bf16),
                pltpu.VMEM((2 * TOK, out_grads.shape[1]), bf16),
                pltpu.VMEM(in_projection.shape, bf16),
                pltpu.VMEM(out_projection.shape, bf16),
                pltpu.SMEM(lengths.shape, jnp.int32),
                pltpu.VMEM(queries.shape, bf16),
                pltpu.VMEM((RANK, IN_PAD), f32),
                pltpu.VMEM((4 * Z * PIECE, TOK), bf16),
                pltpu.VMEM((2, RANK, 2 * TOK), f32),
                pltpu.VMEM((RANK, 2 * TOK), f32),
                pltpu.VMEM((RANK, 2 * TOK), f32),
                pltpu.VMEM((RANK, TOK), f32),
                pltpu.VMEM((2, 8, TOK), f32),
                pltpu.VMEM((4 * Q_ROWS, queries.shape[1]), bf16),
                pltpu.VMEM((Z * TOK, TOK), f32),
                pltpu.VMEM((RANK // 2, TOK), f32),
                pltpu.VMEM((RANK, TOK), f32),
                pltpu.VMEM((3, RANK // 8, TOK), f32),
                pltpu.VMEM((Z - 1, RANK // 8, TOK), f32),
                pltpu.VMEM((Y - 1, RANK // 8, TOK), f32),
                pltpu.VMEM((2, RANK // 8, TOK), f32),
                pltpu.VMEM((RANK // 2, 8 * Z, TOK), f32),
                pltpu.VMEM((8 * Z, TOK), f32),
                pltpu.VMEM((Z, 8, TOK), f32),
                sem((4,)),
                sem((2 * Z,)),
                sem((2 * Z,)),
                sem((2 * Z,)),
                sem((3,)),
                sem((Z,)),
                sem((Z,)),
                sem((2,)),
                sem((2,)),
                sem((Z,)),
                sem((Z,)),
                sem((Z,)),
                sem((Z,)),
                sem((Z,)),
                sem((Z,)),
                sem((6,)),
                sem((2, H, 2)),
                sem((2, H, 2)),
                sem((5,)),
                sem((5,)),
                sem((5, 7)),
                sem((5,)),
            ],
            compiler_params=pltpu.CompilerParams(
                collective_id=0, has_side_effects=True, vmem_limit_bytes=60 * 1024 * 1024
            ),
        )(activations, out_grads, in_projection, out_projection, lengths, queries)

    placed = (
        P(("dp", "query"), None),
        P(("dp", "query"), None),
        P(None, "query"),
        P(None, "query"),
        P(("dp", "query")),
        P("query", None),
    )
    return jax.shard_map(
        on_device, mesh=mesh, in_specs=placed, out_specs=P(("dp", "query"), None), check_vma=False
    )
```

```python
import functools

import jax
import jax.numpy as jnp
from jax import lax
from jax.experimental import pallas as pl
from jax.experimental.pallas import tpu as pltpu
from jax.sharding import PartitionSpec as P

MESH = pl.DeviceIdType.MESH
RANK = 64
SEQ = 16
TOK = 128
IN_COLS = 448
IN_PAD = 512
OUT_COLS = 128
FULL = 384
HALF = RANK // 2
PIECE = 4 * HALF + HALF // 2
Q_ROWS = 32
NT = (((1,), (1,)), ((), ()))
NN = (((1,), (0,)), ((), ()))


def dot(a, b, dims=NN):
    return lax.dot_general(a, b, dims, preferred_element_type=jnp.float32)


def split(x):
    hi = x.astype(jnp.bfloat16)
    return hi, (x - hi.astype(jnp.float32)).astype(jnp.bfloat16)


def inverse_of_four(p):
    a, b, d = p[0][0], p[0][1], p[1][1]
    scale = 1.0 / (a * d - b * b)
    u00, u01, u11 = d * scale, -b * scale, a * scale
    c = [[p[0][2], p[0][3]], [p[1][2], p[1][3]]]
    x = [[u00 * c[0][j] + u01 * c[1][j] for j in range(2)], [u01 * c[0][j] + u11 * c[1][j] for j in range(2)]]
    s00 = p[2][2] - (c[0][0] * x[0][0] + c[1][0] * x[1][0])
    s01 = p[2][3] - (c[0][0] * x[0][1] + c[1][0] * x[1][1])
    s11 = p[3][3] - (c[0][1] * x[0][1] + c[1][1] * x[1][1])
    scale = 1.0 / (s00 * s11 - s01 * s01)
    t00, t01, t11 = s11 * scale, -s01 * scale, s00 * scale
    w = [[x[i][0] * t00 + x[i][1] * t01, x[i][0] * t01 + x[i][1] * t11] for i in range(2)]
    v00 = u00 + w[0][0] * x[0][0] + w[0][1] * x[0][1]
    v01 = u01 + w[0][0] * x[1][0] + w[0][1] * x[1][1]
    v11 = u11 + w[1][0] * x[1][0] + w[1][1] * x[1][1]
    return [
        [v00, v01, -w[0][0], -w[0][1]],
        [v01, v11, -w[1][0], -w[1][1]],
        [-w[0][0], -w[1][0], t00, t01],
        [-w[0][1], -w[1][1], t01, t11],
    ]


def damped_inverses(total, tokens):
    lane = lax.broadcasted_iota(jnp.int32, (RANK, TOK), 1)
    row = lax.broadcasted_iota(jnp.int32, (RANK, TOK), 0)
    column = lane % RANK
    left = lane < RANK
    work = total * (1.0 / tokens)
    diagonal = jnp.where(column == row, work, 0.0)
    trace = jnp.where(left, jnp.sum(jnp.where(left, diagonal, 0.0)), jnp.sum(jnp.where(left, 0.0, diagonal)))
    work = jnp.where(column == row, work + 0.1 * trace / RANK, work)
    first = jnp.where(left, 0, RANK)
    column1 = lax.broadcasted_iota(jnp.int32, (1, TOK), 1) % RANK
    for k in range(0, RANK, 4):
        columns = [jnp.take_along_axis(work, first + (k + i), axis=1) for i in range(4)]
        rows = [work[k + i : k + i + 1] for i in range(4)]
        pivot = inverse_of_four([[columns[j][k + i : k + i + 1] for j in range(4)] for i in range(4)])
        scaled = []
        for i in range(4):
            value = (pivot[i][0] * rows[0] + pivot[i][1] * rows[1]) + (pivot[i][2] * rows[2] + pivot[i][3] * rows[3])
            for j in range(4):
                value = jnp.where(column1 == k + j, pivot[i][j], value)
            scaled.append(value)
        work = jnp.where((column >= k) & (column < k + 4), 0.0, work)
        work = (work - columns[0] * scaled[0] - columns[1] * scaled[1]) - (
            columns[2] * scaled[2] + columns[3] * scaled[3]
        )
        for i in range(4):
            work = jnp.where(row == k + i, scaled[i], work)
    return work


def gather_order(Z):
    H = Z // 2
    times = {d: 4.5 + 0.95 * (H - 1 - d) for d in range(1, H)}
    times[H] = max(times.get(H - 1, 4.5) + 2.5, 7.0)
    order = [(0.3, "near", 0), (5.0, "q", 0), (9.4, "q", 1)]
    for off in [0] + [sign * d for d in range(H - 1, 0, -1) for sign in (-1, 1)] + [H]:
        t = times[abs(off)] if off else 0.0
        if off:
            order += [(t, "z", off), (t + 2.7, "y", off), (t + 2.75, "near", off)]
        order += [(t + 2.7, "c", off), (t + 5.2, "p", off), (t + 5.3, "far", off)]
    return [event[1:] for event in sorted(order, key=lambda event: event[0])]


def far_first(count):
    half = count // 2
    return [half] + [sign * d for d in range(half - 1, 0, -1) for sign in (1, -1)] + [0]


def goes_on(H, dist, way, part):
    return dist + 1 < H or (dist + 1 == H and part == way)


def kernel(
    Y, Z, tokens,
    acts_hbm, outg_hbm, inp_hbm, outp_hbm, len_hbm, q_hbm,
    out_ref,
    acts, outg, inp, outp, lens, qraw, stage, gath, halves, other, both, spare, lives, qall, tok, part, total, ar1, ar2, ar3, mine, gsc, sco, ret,
    loc_sem, act_loc, act_send, act_recv, og_sem, z_send, z_recv, r_send, r_recv, y_send, y_recv, cx_send, cx_recv,
    pt_send, pt_recv, sw_sem,
    t_send, t_recv, q_send, q_recv, a_send, a_recv,
):
    H = Z // 2
    dpi, qi = lax.axis_index("dp"), lax.axis_index("query")
    y, xl = dpi // 2, dpi % 2
    xh, z, c = qi // (2 * Z), (qi // 2) % Z, qi % 2

    def at(y_, xl_, xh_, z_, c_):
        return (y_ * 2 + xl_, xh_ * (2 * Z) + z_ * 2 + c_)

    def zp(off):
        return (z + (off + Z)) % Z

    def z_peer(off):
        return at(y, xl, xh, zp(off), c)

    def y_peer(off):
        return at((y + off) % Y, xl, xh, z, c)

    def x_peer(m):
        return at(y, (xl + (m // 2) % 2) % 2, (xh + m // 4) % 2, z, (c + m % 2) % 2)

    cross = at(y, 1 - xl, 1 - xh, z, c)
    partner = at(y, 1 - xl, xh, z, c)
    sibling = at(y, xl, xh, z, 1 - c)

    pending = []

    def push(ref_src, ref_dst, send, recv, to):
        copy = pltpu.make_async_remote_copy(
            src_ref=ref_src, dst_ref=ref_dst, send_sem=send, recv_sem=recv, device_id=to, device_id_type=MESH
        )
        copy.start()
        pending.append(copy)

    def got(ref, sem):
        pltpu.make_async_copy(ref, ref, sem).wait()

    def settle(keep):
        while len(pending) > keep:
            pending.pop(0).wait_send()

    loads = [
        pltpu.make_async_copy(inp_hbm, inp, loc_sem.at[0]),
        pltpu.make_async_copy(outp_hbm, outp, loc_sem.at[1]),
        pltpu.make_async_copy(q_hbm, qraw, loc_sem.at[2]),
        pltpu.make_async_copy(len_hbm, lens, loc_sem.at[3]),
    ]
    for load in loads:
        load.start()

    barrier = pltpu.get_barrier_semaphore()
    peers = [y_peer(d) for d in range(1, Y)] + [z_peer(d) for d in range(1, Z)] + [x_peer(m) for m in range(7, 0, -1)]
    for peer in peers:
        pl.semaphore_signal(barrier, inc=1, device_id=peer, device_id_type=MESH)

    order = gather_order(Z)
    folds = [event for event in order if event[0] in ("near", "far")]

    def window(name, off):
        return (xh if name == "near" else 1 - xh) * Z + zp(off)

    def act_columns(k, cc):
        return pl.ds(pl.multiple_of(k * (2 * IN_COLS) + cc * (IN_COLS - RANK), 128), IN_PAD)

    def act_slot(k, cc):
        return acts.at[pl.ds(pl.multiple_of(cc * TOK, TOK), TOK), pl.ds(pl.multiple_of(k * IN_PAD, IN_PAD), IN_PAD)]

    def out_slot(cc):
        return outg.at[pl.ds(pl.multiple_of(cc * TOK, TOK), TOK), :]

    mate = at(y + 1 - 2 * (y % 2), xl, xh, z, c)
    side = (y + xl) % 2

    def piece(h, off, p):
        return gath.at[pl.ds(pl.multiple_of((h * Z + zp(off)) * (2 * PIECE) + p * PIECE, 16), PIECE), :]

    def quarter(off, r):
        first = (xh * Z + zp(off)) * (2 * PIECE) + side * PIECE + r * 80
        return gath.at[pl.ds(pl.multiple_of(first, 16), PIECE - 80 if r else 80), :]

    stage[...] = jnp.zeros_like(stage)
    loads[0].wait()
    loads[1].wait()
    stage[:, 0:IN_COLS] = inp[...].astype(jnp.float32)
    plain = stage[...]
    shifted = pltpu.roll(plain, IN_PAD - RANK, 1)
    full = jnp.where(c == 1, shifted[:, 0:FULL], plain[:, 0:FULL])
    tile = jnp.where(c == 1, plain[:, 0:128], plain[:, FULL:IN_PAD])
    lane16 = lax.broadcasted_iota(jnp.int32, (HALF // 2, TOK), 1)

    def block_rows(k, p, first, count):
        return pl.ds(pl.multiple_of(k * (2 * PIECE) + p * PIECE + first, 16), count)

    for p in range(2):
        for j in range(3):
            chunk = full[p * HALF : (p + 1) * HALF, 128 * j : 128 * j + 128]
            gath[block_rows(xh * Z + z, p, j * HALF, HALF), :] = chunk.astype(jnp.bfloat16)
        gath[block_rows(xh * Z + z, p, 3 * HALF, HALF), :] = outp[p * HALF : (p + 1) * HALF, :]
        upper, lower = tile[p * HALF : p * HALF + 16], tile[p * HALF + 16 : (p + 1) * HALF]
        folded = jnp.where(lane16 < RANK, upper, pltpu.roll(lower, RANK, 1))
        gath[block_rows(xh * Z + z, p, 4 * HALF, HALF // 2), :] = folded.astype(jnp.bfloat16)
    pl.semaphore_wait(barrier, len(peers))

    lane_q = lax.broadcasted_iota(jnp.int32, (Q_ROWS, TOK), 1)
    q_cols = qraw.shape[1]

    def q_slot(h, cc):
        return (h * 2 + cc) * Q_ROWS

    def q_piece(h, cc, p):
        half = Q_ROWS // 2
        return qall.at[pl.ds(pl.multiple_of(q_slot(h, cc) + p * half, half), half), :]

    own_q = pl.ds(pl.multiple_of(q_slot(xh, c), Q_ROWS), Q_ROWS)

    def pair_queries():
        loads[2].wait()
        for m in range(q_cols // 256):
            first = qraw[:, 128 * m : 128 * m + 128].astype(jnp.float32)
            second = qraw[:, q_cols // 2 + 128 * m : q_cols // 2 + 128 * m + 128].astype(jnp.float32)
            low = jnp.where(lane_q < RANK, first, pltpu.roll(second, RANK, 1))
            high = jnp.where(lane_q < RANK, pltpu.roll(first, RANK, 1), second)
            qall[own_q, 256 * m : 256 * m + 128] = low.astype(jnp.bfloat16)
            qall[own_q, 256 * m + 128 : 256 * m + 256] = high.astype(jnp.bfloat16)

    sums = [jnp.zeros((RANK, 2 * TOK), jnp.float32), jnp.zeros((RANK, 2 * TOK), jnp.float32)]
    ref = piece(xh, 0, side)
    for d in range(H - 1, 0, -1):
        for sign in (1, -1):
            push(ref, ref, z_send.at[H - 1 + sign * d], z_recv.at[H - 1 - sign * d], z_peer(sign * d))
    push(ref, ref, cx_send.at[H - 1], cx_recv.at[H - 1], cross)
    own_loads = []
    for j, fold in enumerate(folds):
        k = window(*fold)
        own_loads.append(pltpu.make_async_copy(acts_hbm.at[:, act_columns(k, c)], act_slot(k, c), act_loc.at[j]))
        own_loads[-1].start()
        if j == 0:
            out_load = pltpu.make_async_copy(outg_hbm, out_slot(c), og_sem.at[0])
            out_load.start()
    for event in order:
        kind, off = event
        slot = H - 1 + off
        if kind == "z":
            ref = piece(xh, off, side)
            if off == H:
                got(quarter(H, 0), r_recv.at[0])
                got(quarter(H, 1), r_recv.at[1])
            else:
                got(ref, z_recv.at[slot])
            for r, sign in ((0, 1), (1, -1)):
                if off == -sign * (H - 1):
                    relay = quarter(off, r)
                    push(relay, relay, r_send.at[r], r_recv.at[r], z_peer(sign))
            push(ref, ref, cx_send.at[slot], cx_recv.at[slot], cross)
            push(ref, ref, y_send.at[slot], y_recv.at[slot], mate)
        elif kind == "y":
            got(piece(xh, off, 1 - side), y_recv.at[slot])
        elif kind == "c":
            ref = piece(1 - xh, off, 1 - side)
            got(ref, cx_recv.at[slot])
            push(ref, ref, pt_send.at[slot], pt_recv.at[slot], partner)
        elif kind == "p":
            got(piece(1 - xh, off, side), pt_recv.at[slot])
        elif event == ("q", 0):
            ref = q_piece(1 - xh, c, 1 - xl)
            got(ref, q_recv.at[0])
            push(ref, ref, q_send.at[2], q_recv.at[2], partner)
            push(ref, ref, q_send.at[3], q_recv.at[3], sibling)
        elif event == ("q", 1):
            ref = q_piece(1 - xh, c, xl)
            got(ref, q_recv.at[2])
            push(ref, ref, q_send.at[4], q_recv.at[4], sibling)
        else:
            j = folds.index(event)
            if j == 0:
                for i, fold in enumerate(folds):
                    k = window(*fold)
                    push(acts_hbm.at[:, act_columns(k, 1 - c)], act_slot(k, c), act_send.at[i], act_recv.at[i], sibling)
                    if i == 0:
                        push(outg_hbm, out_slot(c), og_sem.at[1], og_sem.at[2], sibling)
                pair_queries()
                ref = q_piece(xh, c, xl)
                push(ref, ref, q_send.at[0], q_recv.at[0], cross)
                ref = qall.at[own_q, :]
                push(ref, ref, q_send.at[1], q_recv.at[1], sibling)
                lane1 = lax.broadcasted_iota(jnp.int32, (8, TOK), 1)
                counts = jnp.zeros((8, TOK), jnp.int32)
                loads[3].wait()
                for e in range(TOK // SEQ):
                    counts = jnp.where(lane1 // SEQ == e, lens[e], counts)
                lives[c] = (lane1 % SEQ < counts).astype(jnp.float32)
                push(lives.at[c], lives.at[c], sw_sem.at[2], sw_sem.at[3], sibling)
                out_load.wait()
                got(out_slot(1 - c), og_sem.at[2])
            k = window(*event)
            own_loads[j].wait()
            got(act_slot(k, 1 - c), act_recv.at[j])
            weights = [
                jnp.concatenate([gath[block_rows(k, p, j * HALF, HALF), :] for p in range(2)], axis=0) for j in range(4)
            ]
            last = []
            for p in range(2):
                folded = gath[block_rows(k, p, 4 * HALF, HALF // 2), :].astype(jnp.float32)
                turned = pltpu.roll(folded, RANK, 1)
                for straight in (0, 1):
                    last.append(jnp.where(lane16 // RANK == c, jnp.where(c == straight, folded, turned), 0.0))
            last = jnp.concatenate(last, axis=0).astype(jnp.bfloat16)
            whole = acts[:, pl.ds(pl.multiple_of(k * IN_PAD + c * 128, 128), FULL)]
            tile = acts[:, pl.ds(pl.multiple_of(k * IN_PAD + (1 - c) * FULL, 128), 128)]
            weight = jnp.concatenate(weights[0:3] + [last], axis=1)
            sums[0] = sums[0] + dot(weight, jnp.concatenate([whole, tile], axis=1), NT)
            columns = pl.ds(pl.multiple_of(k * (2 * OUT_COLS) + c * OUT_COLS, OUT_COLS), OUT_COLS)
            sums[1] = sums[1] + dot(weights[3], outg[:, columns], NT)

    halves[0] = sums[0]
    halves[1] = sums[1]
    push(halves.at[1 - c], other, sw_sem.at[0], sw_sem.at[1], sibling)
    got(lives.at[1 - c], sw_sem.at[3])
    live = jnp.concatenate([lives[0, 0:1, :], lives[1, 0:1, :]], axis=1)
    got(other, sw_sem.at[1])
    masked = (halves[c] + other[...]) * live
    both[...] = masked
    hi, lo = split(masked)
    hi_lo = jnp.concatenate([hi, lo], axis=1)
    twice = jnp.concatenate([hi_lo, hi_lo], axis=0)
    lo_hi = jnp.concatenate([lo, hi], axis=1)
    gram = dot(hi_lo, twice, NT) + dot(lo_hi, twice, NT)
    half = RANK // 2
    lane = lax.broadcasted_iota(jnp.int32, (half, TOK), 1)
    part[...] = jnp.where(lane < RANK, gram[0:half], gram[half:])

    rows_x = half // 4

    def x_rows(m):
        index = ((xh + m // 4) % 2) * 2 + (xl + (m // 2) % 2) % 2
        return pl.ds(pl.multiple_of(index * rows_x, rows_x), rows_x)

    def tok_piece(zz, p):
        return tok.at[pl.ds(pl.multiple_of(zz * TOK + p * RANK, RANK), RANK), :]

    def tok_step(dist):
        for way, sign in ((0, -1), (1, 1)):
            for p in (0, 1):
                ref = tok_piece(zp(sign * dist), p)
                if dist == H and p != way:
                    continue
                if dist > 0:
                    got(ref, t_recv.at[way, dist - 1, p])
                if goes_on(H, dist, way, p):
                    push(ref, ref, t_send.at[way, dist, p], t_recv.at[way, dist, p], z_peer(-sign))

    for j, m in enumerate((4, 6, 2)):
        push(part.at[x_rows(m), :], ar1.at[j], a_send.at[0, j], a_recv.at[0], x_peer(m))
    for cc in range(2):

        @pl.when(c == cc)
        def _():
            tok[pl.ds(pl.multiple_of(z * TOK + cc * RANK, RANK), RANK), :] = both[:, cc * TOK : (cc + 1) * TOK]
            spare[...] = both[:, (1 - cc) * TOK : (2 - cc) * TOK]

    push(spare, tok_piece(z, c), sw_sem.at[4], sw_sem.at[5], sibling)
    got(tok_piece(z, 1 - c), sw_sem.at[5])
    tok_step(0)
    settle(30)
    got(ar1, a_recv.at[0])
    summed = part[x_rows(0), :]
    for j in range(3):
        summed = summed + ar1[j]
    mine[0] = summed
    for d in [off % Z for off in far_first(Z)[:-1]]:
        push(mine.at[0], ar2.at[d - 1], a_send.at[1, d - 1], a_recv.at[1], z_peer(d))
    settle(25)
    tok_step(1)
    got(ar2, a_recv.at[1])
    for d in range(Z - 1):
        summed = summed + ar2[d]
    mine[1] = summed
    for d in [off % Y for off in far_first(Y)[:-1]]:
        push(mine.at[1], ar3.at[d - 1], a_send.at[2, d - 1], a_recv.at[2], y_peer(d))
    if H > 2:
        tok_step(2)
    settle(25)
    got(ar3, a_recv.at[2])
    for d in range(Y - 1):
        summed = summed + ar3[d]

    def total_rows(cc):
        return total.at[pl.ds(pl.multiple_of((cc * 4 + xh * 2 + xl) * rows_x, rows_x), rows_x), :]

    here = total_rows(c)
    here[...] = summed
    for m in (5, 7, 4, 6, 3, 2, 1):
        push(here, here, a_send.at[3, m - 1], a_recv.at[3], x_peer(m))
    if H > 3:
        tok_step(3)
    settle(15)
    got(total.at[0 : RANK - rows_x, :], a_recv.at[3])
    if H > 1:
        tok_step(H)

    ins, outs = total[0:half], total[half:]
    sides = jnp.concatenate(
        [
            jnp.where(lane < RANK, ins, pltpu.roll(outs, RANK, 1)),
            jnp.where(lane < RANK, pltpu.roll(ins, RANK, 1), outs),
        ],
        axis=0,
    )
    inverses = damped_inverses(sides, tokens)
    lane = lax.broadcasted_iota(jnp.int32, (RANK, TOK), 1)
    blocks = jnp.concatenate(
        [jnp.where(lane < RANK, inverses, 0.0), jnp.where(lane < RANK, 0.0, inverses)], axis=0
    )
    hi, lo = split(blocks)
    blocks = jnp.concatenate([hi, lo, hi], axis=1)
    example = lax.broadcasted_iota(jnp.int32, (SEQ // 2, TOK), 0)
    token = lax.broadcasted_iota(jnp.int32, (SEQ // 2, TOK), 1)
    belongs = (token // SEQ == example).astype(jnp.float32)
    nothing = jnp.zeros((RANK, TOK), jnp.bfloat16)
    got(qall.at[pl.ds(pl.multiple_of(q_slot(xh, 1 - c), Q_ROWS), Q_ROWS), :], q_recv.at[1])
    got(q_piece(1 - xh, 1 - c, 1 - xl), q_recv.at[3])
    got(q_piece(1 - xh, 1 - c, xl), q_recv.at[4])
    offs = far_first(Z)
    group = Z // 2
    for k in range(Z):
        if k % 2 == 0:
            rows = [
                split(tok[pl.ds(pl.multiple_of(zp(off) * TOK, TOK), TOK), :]) for off in offs[k : k + 2]
            ]
            hi = jnp.concatenate([rows[0][0], rows[1][0]], axis=1)
            lo = jnp.concatenate([rows[0][1], rows[1][1]], axis=1)
            pair = dot(blocks, jnp.concatenate([hi, hi, lo], axis=0))
        ins, outs = pair[0:RANK, (k % 2) * TOK : (k % 2 + 1) * TOK], pair[RANK:, (k % 2) * TOK : (k % 2 + 1) * TOK]
        left, right = [], []
        for w in split(outs):
            spread = (w.astype(jnp.float32)[:, None, :] * belongs[None, :, :]).astype(jnp.bfloat16)
            spread = spread.reshape(RANK * 8, TOK)
            left.append(jnp.concatenate([spread[0 : half * 8], spread[half * 8 :]], axis=1))
        for w in split(ins):
            right += [jnp.concatenate([w, nothing], axis=1), jnp.concatenate([nothing, w], axis=1)]
        grads = dot(left[0], jnp.concatenate(right, axis=0), NT)
        grads = grads[:, 0:TOK] + (grads[:, TOK:] + dot(left[1], jnp.concatenate(right[0:2], axis=0), NT))
        gsc[:, k * 8 : (k + 1) * 8, :] = grads.reshape(half, 8, TOK)
        if (k + 1) % group:
            continue
        first = k + 1 - group
        scores = jnp.zeros((2 * 8 * group, TOK), jnp.float32)
        for m in range(half // 2):
            mine_both = [gsc[2 * m + i, first * 8 : (k + 1) * 8, :] for i in range(2)]
            hi, lo = split(jnp.concatenate(mine_both, axis=1))
            scores = scores + dot(jnp.concatenate([hi, lo], axis=0), qall[:, 256 * m : 256 * m + 256], NT)
        sco[first * 8 : (k + 1) * 8, :] = scores[0 : 8 * group] + scores[8 * group :]
        for j in range(first, k + 1):
            if offs[j] == 0:
                ret[0] = sco[j * 8 : (j + 1) * 8, :]
            else:
                d = offs[j] % Z
                push(sco.at[j * 8 : (j + 1) * 8, :], ret.at[d], a_send.at[4, d - 1], a_recv.at[4], z_peer(d))
    settle(Z // 2 - 1)
    got(ret.at[1:Z], a_recv.at[4])
    lane8 = lax.broadcasted_iota(jnp.int32, (8, TOK), 1)
    width = Z * RANK
    for m in range(Z // 2):
        first = ret[zp(-2 * m)]
        second = ret[zp(-2 * m - 1)]
        out_ref[:, 128 * m : 128 * m + 128] = jnp.where(lane8 < RANK, first, pltpu.roll(second, RANK, 1))
        out_ref[:, width + 128 * m : width + 128 * m + 128] = jnp.where(
            lane8 < RANK, pltpu.roll(first, RANK, 1), second
        )
    settle(0)


def solution(mesh):
    Y, Z = mesh.shape["dp"] // 2, mesh.shape["query"] // 4
    H = Z // 2

    def on_device(activations, out_grads, in_projection, out_projection, lengths, queries):
        tokens = activations.shape[0] * mesh.shape["dp"] * mesh.shape["query"]
        f32, bf16 = jnp.float32, jnp.bfloat16
        sem = pltpu.SemaphoreType.DMA
        return pl.pallas_call(
            functools.partial(kernel, Y, Z, tokens),
            out_shape=pltpu.VMEM((lengths.shape[0], Z * 4 * Q_ROWS), f32),
            in_specs=[pl.BlockSpec(memory_space=pltpu.HBM)] * 6,
            out_specs=pl.BlockSpec(memory_space=pltpu.VMEM),
            scratch_shapes=[
                pltpu.VMEM((2 * TOK, 2 * Z * IN_PAD), bf16),
                pltpu.VMEM((2 * TOK, out_grads.shape[1]), bf16),
                pltpu.VMEM(in_projection.shape, bf16),
                pltpu.VMEM(out_projection.shape, bf16),
                pltpu.SMEM(lengths.shape, jnp.int32),
                pltpu.VMEM(queries.shape, bf16),
                pltpu.VMEM((RANK, IN_PAD), f32),
                pltpu.VMEM((4 * Z * PIECE, TOK), bf16),
                pltpu.VMEM((2, RANK, 2 * TOK), f32),
                pltpu.VMEM((RANK, 2 * TOK), f32),
                pltpu.VMEM((RANK, 2 * TOK), f32),
                pltpu.VMEM((RANK, TOK), f32),
                pltpu.VMEM((2, 8, TOK), f32),
                pltpu.VMEM((4 * Q_ROWS, queries.shape[1]), bf16),
                pltpu.VMEM((Z * TOK, TOK), f32),
                pltpu.VMEM((RANK // 2, TOK), f32),
                pltpu.VMEM((RANK, TOK), f32),
                pltpu.VMEM((3, RANK // 8, TOK), f32),
                pltpu.VMEM((Z - 1, RANK // 8, TOK), f32),
                pltpu.VMEM((Y - 1, RANK // 8, TOK), f32),
                pltpu.VMEM((2, RANK // 8, TOK), f32),
                pltpu.VMEM((RANK // 2, 8 * Z, TOK), f32),
                pltpu.VMEM((8 * Z, TOK), f32),
                pltpu.VMEM((Z, 8, TOK), f32),
                sem((4,)),
                sem((2 * Z,)),
                sem((2 * Z,)),
                sem((2 * Z,)),
                sem((3,)),
                sem((Z,)),
                sem((Z,)),
                sem((2,)),
                sem((2,)),
                sem((Z,)),
                sem((Z,)),
                sem((Z,)),
                sem((Z,)),
                sem((Z,)),
                sem((Z,)),
                sem((6,)),
                sem((2, H, 2)),
                sem((2, H, 2)),
                sem((5,)),
                sem((5,)),
                sem((5, 7)),
                sem((5,)),
            ],
            compiler_params=pltpu.CompilerParams(
                collective_id=0, has_side_effects=True, vmem_limit_bytes=60 * 1024 * 1024
            ),
        )(activations, out_grads, in_projection, out_projection, lengths, queries)

    placed = (
        P(("dp", "query"), None),
        P(("dp", "query"), None),
        P(None, "query"),
        P(None, "query"),
        P(("dp", "query")),
        P("query", None),
    )
    return jax.shard_map(
        on_device, mesh=mesh, in_specs=placed, out_specs=P(("dp", "query"), None), check_vma=False
    )
```
